128 devices in a mesh: pfx: 16 (over x, z), tp: 8 (over y, core).
Axes of the slice: x: 4, y: 4, z: 4, core: 2. Of those that a mesh axis runs over, the one named last changes fastest.
Arguments:
- queries: bfloat16 [512, 16384], P('pfx', 'tp'), may hold values from -8 to 8
- route: int32 [512], P('pfx'), may hold values from 0 to 15, as said below
- place: int32 [16], replicated, may hold values from 0 to 15, each once
- suffix_len: int32 [512], P('pfx'), may hold values from 1 to 256, as said below
- prefix_keys: bfloat16 [131072, 1024], P('pfx', 'tp'), may hold values from -8 to 8
- prefix_values: bfloat16 [131072, 1024], P('pfx', 'tp'), may hold values from -6 to 6
- suffix_keys: bfloat16 [512, 256, 1024], P('pfx', None, 'tp'), may hold values from -8 to 8
- suffix_values: bfloat16 [512, 256, 1024], P('pfx', None, 'tp'), may hold values from -6 to 6
- out_weight: bfloat16 [16384, 16384], P('tp', 'pfx'), may hold values from -0.1875 to 0.1875
Outputs:
- mixture: bfloat16 [512, 16384], P('tp', 'pfx')
The draws below stay inside these ranges and needn't reach their ends.
Inputs may be any that keep to these rules, and one draw needn't show every extreme that they name: `route`: within the rows of one device (aligned blocks of 32 requests) no prefix is named more than 6 times, and one prefix is named exactly 6 times in every block. Prefix p's cache rows start at place[p] * 8192. `suffix_len`: every aligned block of 32 requests holds one of length 256.
All inputs are finite; a program needn't handle non-finite values.
Results may differ from the reference program's by a relative error of at most 0.019.
Values may be sent and summed in bfloat16 or wider, within the bound.
No kernel may reach another device: no remote copies, remote signals or barrier semaphores. Data moves between devices by JAX's collectives and lax.ppermute only.
A program may use at most 128 MiB of HBM per device.

```python
import jax
import jax.numpy as jnp
from jax import lax

D = 16384
HEADS = 128
KVH = 8
HDIM = 128
R_DEV = 32
PLEN = 8192
SMAX = 256
NPFX = 16
REQS = 512
CAP = 6


def draw_route(key, part):
    key = jax.random.fold_in(key, 11)
    hot_key, pick_key = jax.random.split(key)
    hottest = jax.random.randint(hot_key, (), 0, NPFX, dtype=jnp.int32)
    others = jnp.arange((NPFX - 1) * CAP, dtype=jnp.int32) // CAP
    others = others + (others >= hottest).astype(jnp.int32)

    def one_block(block_key):
        first_key, second_key = jax.random.split(block_key)
        chosen = jax.random.permutation(first_key, others)[:R_DEV - CAP]
        block_row = jnp.concatenate([jnp.full((CAP,), hottest, jnp.int32), chosen])
        return jax.random.permutation(second_key, block_row)
    block_keys = jax.random.split(pick_key, REQS // R_DEV)
    return jax.vmap(one_block)(block_keys).reshape(REQS).astype(jnp.int32)


def draw_suffix_len(key, part):
    key = jax.random.fold_in(key, 23)
    first_key, second_key = jax.random.split(key)
    blocks = REQS // R_DEV
    lengths = jax.random.randint(first_key, (blocks, R_DEV), 1, SMAX + 1, dtype=jnp.int32)
    longest = jax.random.randint(second_key, (blocks, 1), 0, R_DEV, dtype=jnp.int32)
    column = jnp.arange(R_DEV, dtype=jnp.int32)[None, :]
    return jnp.where(column == longest, SMAX, lengths).astype(jnp.int32).reshape(REQS)


def draw_queries(key, part):
    key = jax.random.fold_in(key, 37)
    first_key = jax.random.fold_in(key, 0)
    values = jax.random.normal(first_key, (REQS, HEADS * HDIM), jnp.float32)
    return jnp.clip(values, -8.0, 8.0).astype(jnp.bfloat16)


def draw_prefix_keys(key, part):
    key = jax.random.fold_in(key, 41)
    values = jax.random.normal(key, (NPFX * PLEN, KVH * HDIM), jnp.float32)
    values = jnp.clip(values, -6.0, 6.0)
    return values.astype(jnp.bfloat16)


def draw_suffix_keys(key, part):
    key = jax.random.fold_in(key, 53)
    values = jax.random.normal(key, (REQS, SMAX, KVH * HDIM), jnp.float32)
    values = 2.5 * jnp.clip(values, -3.2, 3.2)
    return values.astype(jnp.bfloat16)


def block_levels(stream_key, shape, pieces, least, top_value):
    loudness, own = 1.0, jax.random.fold_in(stream_key, 6)
    for dim, parts in pieces:
        heights = jnp.exp(jax.random.uniform(jax.random.fold_in(own, dim), (parts,), jnp.float32, least / len(pieces), top_value / len(pieces)))
        loudness = loudness * jnp.repeat(heights, shape[dim] // parts).reshape([-1 if axis == dim else 1 for axis in range(len(shape))])
    return loudness


def gaussian(stream_key, dims, scale, most, pieces=(), kind=jnp.bfloat16):
    drawn = scale * jax.random.normal(stream_key, dims, jnp.float32)
    if pieces:
        drawn = drawn * block_levels(stream_key, dims, pieces, -0.22, 0.18)
    return jnp.clip(drawn, -most, most).astype(kind)


def setup_inputs(seed: int = 0) -> dict:
    splits = jax.random.split(jax.random.key(seed), 10)
    queries = draw_queries(jax.random.fold_in(splits[9], 71), 0)
    route = draw_route(jax.random.fold_in(splits[9], 71), 0)
    place = jax.random.permutation(splits[2], NPFX).astype(jnp.int32)
    suffix_len = draw_suffix_len(jax.random.fold_in(splits[9], 71), 0)
    prefix_keys = draw_prefix_keys(jax.random.fold_in(splits[9], 71), 0)
    prefix_values = gaussian(splits[5], (NPFX * PLEN, KVH * HDIM), 1.0, 6.0, ((0, 16), (1, 8)))
    suffix_keys = draw_suffix_keys(jax.random.fold_in(splits[9], 71), 0)
    suffix_values = gaussian(splits[7], (REQS, SMAX, KVH * HDIM), 1.0, 6.0, ((0, 16), (2, 8)))
    out_weight = gaussian(splits[8], (HEADS * HDIM, D), (HEADS * HDIM // 16) ** -0.5, 0.1875, ((0, 8), (1, 16)))
    return dict(queries=queries, route=route, place=place, suffix_len=suffix_len, prefix_keys=prefix_keys, prefix_values=prefix_values, suffix_keys=suffix_keys, suffix_values=suffix_values, out_weight=out_weight)


def soft_parts(scores):
    row_top = jnp.max(scores, axis=-1, keepdims=True)
    exponent = jnp.exp(scores - row_top)
    totals = jnp.sum(exponent, axis=-1)
    weights = exponent.astype(jnp.bfloat16)
    return weights, totals, row_top[..., 0] + jnp.log(totals)


def reference(queries, route, place, suffix_len, prefix_keys, prefix_values, suffix_keys, suffix_values, out_weight):
    group_size = HEADS // KVH
    score_scale = HDIM ** -0.5
    slot_of = place[route].astype(jnp.int32)

    def one_request(item):
        query, slot_index, length, keys_own, values_own = item
        query_heads = query.astype(jnp.float32).reshape(KVH, group_size, HDIM)
        begin = (slot_index * PLEN).astype(jnp.int32)
        keys_shared = lax.dynamic_slice_in_dim(prefix_keys, begin, PLEN, 0).astype(jnp.float32).reshape(PLEN, KVH, HDIM)
        values_shared = lax.dynamic_slice_in_dim(prefix_values, begin, PLEN, 0).astype(jnp.float32).reshape(PLEN, KVH, HDIM)
        scores = jnp.einsum('kgd,lkd->kgl', query_heads, keys_shared) * score_scale
        weights, totals, prefix_lse = soft_parts(scores)
        prefix_out = (jnp.einsum('kgl,lkd->kgd', weights.astype(jnp.float32), values_shared) / totals[..., None]).astype(jnp.bfloat16)
        keys_local = keys_own.astype(jnp.float32).reshape(SMAX, KVH, HDIM)
        values_local = values_own.astype(jnp.float32).reshape(SMAX, KVH, HDIM)
        scores_own = jnp.einsum('kgd,lkd->kgl', query_heads, keys_local) * score_scale
        live_mask = jnp.arange(SMAX) < length
        scores_own = jnp.where(live_mask, scores_own, -1e30)
        weights_own, totals_own, suffix_lse = soft_parts(scores_own)
        suffix_out = jnp.einsum('kgl,lkd->kgd', weights_own.astype(jnp.float32), values_local) / totals_own[..., None]
        total_lse = jnp.logaddexp(prefix_lse, suffix_lse)
        merged = jnp.exp(prefix_lse - total_lse)[..., None] * prefix_out.astype(jnp.float32) + jnp.exp(suffix_lse - total_lse)[..., None] * suffix_out
        return merged.astype(jnp.bfloat16).reshape(HEADS * HDIM)

    attention = lax.map(one_request, (queries, slot_of, suffix_len, suffix_keys, suffix_values), batch_size=4)
    mixture = jnp.dot(attention.astype(jnp.float32), out_weight.astype(jnp.float32))
    return mixture.astype(jnp.bfloat16)
```

```python
import functools

import jax
import jax.numpy as jnp
from jax import lax
from jax.experimental import pallas as pl
from jax.experimental.pallas import tpu as pltpu
from jax.sharding import PartitionSpec as P

HDIM = 128
SLOTS = 8
CAP = 6
LOG2E = 1.4426950408889634
LN2 = 0.6931471805599453
F32 = jnp.float32
BF16 = jnp.bfloat16
VMEM = pl.BlockSpec(memory_space=pltpu.VMEM)
SMEM = pl.BlockSpec(memory_space=pltpu.SMEM)
PARAMS = pltpu.CompilerParams(vmem_limit_bytes=48 * 2**20)
NT = (((1,), (1,)), ((), ()))


def iota(shape, dim):
    return lax.broadcasted_iota(jnp.int32, shape, dim)


def one_hot(condition):
    return jnp.where(condition, 1.0, 0.0).astype(BF16)


def dest_rows(route_ref, place_ref, count_ref, add):
    for owner in range(place_ref.shape[0]):
        count_ref[owner] = 0
    for r in range(route_ref.shape[0]):
        owner = place_ref[route_ref[r]]
        rank = count_ref[owner]
        count_ref[owner] = rank + 1
        add(r, owner * SLOTS + rank)


def pack_kernel(route_ref, place_ref, q_ref, out_ref, count_ref):
    rows = q_ref.shape[0]
    lane = iota((SLOTS, 128), 1)
    dest = [jnp.full((SLOTS, 128), -1, jnp.int32)]

    def add(r, row):
        dest[0] = jnp.where(lane == r, row, dest[0])

    dest_rows(route_ref, place_ref, count_ref, add)
    pick = one_hot(iota((out_ref.shape[0], rows), 0) == dest[0][:1, :rows])
    out_ref[...] = jnp.dot(pick, q_ref[...], preferred_element_type=F32).astype(BF16)


def suffix_kernel(
    route_ref, place_ref, len_ref, q_ref, k_ref, v_ref, out_ref, lse_ref, dest_ref, count_ref
):
    requests, cache, depth = k_ref.shape
    heads = q_ref.shape[1] // depth
    batch = 16
    dest = [jnp.zeros((requests, 128), jnp.int32)]
    row = iota((requests, 128), 0)

    def add(r, place):
        dest[0] = jnp.where(row == r, place, dest[0])

    dest_rows(route_ref, place_ref, count_ref, add)
    dest_ref[...] = dest[0]
    for b in range(requests // batch):
        first = b * batch
        sl = slice(first, first + batch)
        q = jnp.concatenate([q_ref[sl, h * depth : (h + 1) * depth] for h in range(heads)], axis=0)
        own = iota((batch, 128), 0)
        live = jnp.zeros((batch, 128), jnp.int32)
        for r in range(batch):
            live = jnp.where(own == r, len_ref[first + r], live)
        keys = k_ref[sl].reshape(batch * cache, depth)
        values = v_ref[sl].reshape(batch * cache, depth)
        scores = lax.dot_general(q, keys, NT, preferred_element_type=F32)
        column = iota((batch, batch * cache), 1)
        start = iota((batch, batch * cache), 0) * cache
        inside = (column >= start) & (column < start + live[:, :1])
        bias = jnp.where(inside, 0.0, -jnp.inf)
        scores = scores * (depth**-0.5 * LOG2E) + jnp.concatenate([bias] * heads, axis=0)
        top = jnp.max(scores, axis=1, keepdims=True)
        weights = jnp.exp2(scores - top).astype(BF16)
        both = jnp.dot(
            weights,
            jnp.concatenate([values, jnp.ones_like(values)], axis=1),
            preferred_element_type=F32,
        )
        total = both[:, depth:]
        out = both[:, :depth] / total
        lse = top * LN2 + jnp.log(total)
        for h in range(heads):
            part = slice(h * batch, (h + 1) * batch)
            out_ref[sl, h * depth : (h + 1) * depth] = out[part]
            lse_ref[sl, h * depth : (h + 1) * depth] = lse[part]


KEYS = 4096
COLS = 512


def prefix_kernel(recv_ref, k_ref, v_ref, out_ref, q_ref, acc_ref, top_ref):
    depth = k_ref.shape[1]
    heads = recv_ref.shape[1] // depth
    sources = recv_ref.shape[0] // SLOTS
    items = sources * CAP
    rows = heads * items
    item = iota((items, recv_ref.shape[0]), 0)
    pick = one_hot(iota(item.shape, 1) == item // CAP * SLOTS + item % CAP)
    scale = depth**-0.5 * LOG2E
    for h in range(heads):
        q = jnp.dot(
            pick, recv_ref[:, h * depth : (h + 1) * depth], preferred_element_type=F32
        )
        q = q * scale
        high = q.astype(BF16)
        part = slice(h * items, (h + 1) * items)
        q_ref[part, :depth] = high
        q_ref[part, depth:] = (q - high.astype(F32)).astype(BF16)

    def scores_of(i, c):
        keys = k_ref[pl.ds(i * KEYS, KEYS), :]
        return lax.dot_general(
            jnp.concatenate([keys, keys], axis=1),
            q_ref[pl.ds(c * COLS, COLS), :],
            NT,
            preferred_element_type=F32,
        )

    def value_rows(i):
        values = v_ref[pl.ds(i * KEYS, KEYS), :]
        return jnp.concatenate([values.T, jnp.ones((16, KEYS), BF16)], axis=0)

    steps = k_ref.shape[0] // KEYS
    blocks = rows // COLS
    acc_ref[...] = jnp.zeros_like(acc_ref)

    def step(i, carry):
        turned = value_rows(i)
        for c in range(blocks):
            weights = jnp.exp2(scores_of(i, c)).astype(BF16)
            acc_ref[:, c * COLS : (c + 1) * COLS] += jnp.dot(
                turned, weights, preferred_element_type=F32
            )
        return carry

    lax.fori_loop(0, steps, step, 0)
    top_ref[...] = jnp.zeros_like(top_ref)
    total = acc_ref[depth : depth + 1, :]
    fine = (total > 2.0**-64) & (total < 2.0**100)

    @pl.when(jnp.min(jnp.where(fine, 1.0, 0.0)) < 0.5)
    def _():
        for c in range(blocks):
            sl = slice(c * COLS, (c + 1) * COLS)

            def find(i, top):
                return jnp.maximum(top, jnp.max(scores_of(i, c), axis=0, keepdims=True))

            top = lax.fori_loop(0, steps, find, jnp.full((1, COLS), -jnp.inf, F32))
            top_ref[:, sl] = jnp.broadcast_to(top, (8, COLS))
            acc_ref[:, sl] = jnp.zeros((acc_ref.shape[0], COLS), F32)

            def again(i, carry):
                weights = jnp.exp2(scores_of(i, c) - top).astype(BF16)
                acc_ref[:, sl] += jnp.dot(value_rows(i), weights, preferred_element_type=F32)
                return carry

            lax.fori_loop(0, steps, again, 0)

    total = acc_ref[depth : depth + 1, :]
    inverse = 1.0 / total
    lse = top_ref[:1, :] * LN2 + jnp.log(total)
    high = lse.astype(BF16).astype(F32)
    middle = (lse - high).astype(BF16).astype(F32)
    low = lse - high - middle
    wide = iota((8, rows), 0)
    pieces = jnp.where(wide == 0, high, jnp.where(wide == 1, middle, low))
    row = iota((recv_ref.shape[0], items), 0)
    column = iota(row.shape, 1)
    result_row = one_hot(row == column // CAP * SLOTS + column % CAP)
    lse_row = one_hot(row == column // CAP * SLOTS + CAP)
    spread = jnp.concatenate([result_row, lse_row], axis=1)
    offset = iota((items, depth), 1) - 3 * (iota((items, depth), 0) % CAP)
    for h in range(heads):
        part = slice(h * items, (h + 1) * items)
        out = (acc_ref[:depth, part] * inverse[:, part]).T
        three = pieces[:, part].T
        packed = jnp.where(
            offset == 0,
            three[:, 0:1],
            jnp.where(
                offset == 1, three[:, 1:2], jnp.where(offset == 2, three[:, 2:3], 0.0)
            ),
        )
        both = jnp.concatenate([out.astype(BF16), packed.astype(BF16)], axis=0)
        out_ref[:, h * depth : (h + 1) * depth] = jnp.dot(
            spread, both, preferred_element_type=F32
        ).astype(BF16)


def merge_kernel(back_ref, dest_ref, suffix_ref, lse_ref, out_ref):
    copies, requests, width = out_ref.shape
    depth = HDIM
    dest = dest_ref[:, :1]
    column = iota((requests, back_ref.shape[0]), 1)
    pick_out = one_hot(column == dest)
    pick_lse = one_hot(column == dest // SLOTS * SLOTS + CAP)
    offset = iota((requests, depth), 1) - 3 * (dest % SLOTS)
    mine = (offset >= 0) & (offset < 3)
    for h in range(width // depth):
        sl = slice(h * depth, (h + 1) * depth)
        prefix = jnp.dot(pick_out, back_ref[:, sl], preferred_element_type=F32)
        pieces = jnp.dot(pick_lse, back_ref[:, sl], preferred_element_type=F32)
        prefix_lse = jnp.sum(jnp.where(mine, pieces, 0.0), axis=1, keepdims=True)
        suffix_lse = lse_ref[:, sl]
        top = jnp.maximum(prefix_lse, suffix_lse)
        prefix_part = jnp.exp(prefix_lse - top)
        suffix_part = jnp.exp(suffix_lse - top)
        merged = (prefix_part * prefix + suffix_part * suffix_ref[:, sl]) / (
            prefix_part + suffix_part
        )
        merged = merged.astype(BF16)
        for copy in range(copies):
            out_ref[copy, :, sl] = merged


def project_kernel(core_ref, a_ref, w_ref, mine_ref, other_ref):
    core = core_ref[0]
    block = a_ref.shape[0] // 8
    order = [(y, core) for y in range(4)] + [(y, 1 - core) for y in range(4)]
    a = jnp.concatenate(
        [a_ref[pl.ds(pl.multiple_of((2 * y + c) * block, block), block), :] for y, c in order],
        axis=0,
    )
    half = a.shape[0] // 2
    tile = 256
    for n in range(w_ref.shape[1] // tile):
        sl = slice(n * tile, (n + 1) * tile)
        out = jnp.dot(a, w_ref[:, sl], preferred_element_type=F32)
        mine_ref[:, sl] = out[:half]
        other_ref[:, sl] = out[half:].astype(BF16)


def pair_kernel(y_ref, mine_ref, got_ref, own_ref, one_ref, two_ref, three_ref):
    y = y_ref[0]
    block = own_ref.shape[0]

    def part(k):
        start = pl.multiple_of(lax.rem(y + k, 4) * block, block)
        return mine_ref[pl.ds(start, block), :] + got_ref[pl.ds(start, block), :].astype(F32)

    one_ref[...] = part(1).astype(BF16)
    two_ref[...] = part(2).astype(BF16)
    three_ref[...] = part(3).astype(BF16)
    own_ref[...] = part(0)


def sum_kernel(own_ref, one_ref, two_ref, three_ref, out_ref):
    out_ref[...] = (
        own_ref[...]
        + one_ref[...].astype(F32)
        + two_ref[...].astype(F32)
        + three_ref[...].astype(F32)
    ).astype(BF16)


def call(kernel, outs, specs, scratch=(), cost=None):
    shapes = [jax.ShapeDtypeStruct(shape, dtype) for shape, dtype in outs]
    many = len(shapes) > 1
    return pl.pallas_call(
        kernel,
        out_shape=shapes if many else shapes[0],
        in_specs=specs,
        out_specs=[VMEM] * len(shapes) if many else VMEM,
        scratch_shapes=list(scratch),
        compiler_params=PARAMS,
        cost_estimate=cost,
    )


def on_device(
    queries, route, place, suffix_len, prefix_keys, prefix_values, suffix_keys, suffix_values, out_weight
):
    requests, width = queries.shape
    owners = lax.axis_size("pfx")
    heads = width // HDIM
    buffer_rows = owners * SLOTS
    rows = owners * CAP * heads
    count = pltpu.SMEM((owners,), jnp.int32)
    tp = lax.axis_index("tp")
    core, y = (tp % 2).reshape(1), (tp // 2).reshape(1)

    def exchange(x):
        shape = x.shape
        x = lax.all_to_all(
            x.reshape(owners, -1, width), "pfx", split_axis=0, concat_axis=0, tiled=True
        )
        return x.reshape(shape)

    packed = call(pack_kernel, [((buffer_rows, width), BF16)], [SMEM, SMEM, VMEM], [count])(
        route, place, queries
    )
    received = exchange(packed)
    suffix_out, suffix_lse, dest = call(
        suffix_kernel,
        [((requests, width), F32), ((requests, width), F32), ((requests, 128), jnp.int32)],
        [SMEM, SMEM, SMEM, VMEM, VMEM, VMEM],
        [count],
        pl.CostEstimate(flops=2 * 10**9, bytes_accessed=5 * 10**6, transcendentals=2 * 10**6),
    )(route, place, suffix_len, queries, suffix_keys, suffix_values)
    prefix = call(
        prefix_kernel,
        [((buffer_rows, width), BF16)],
        [VMEM, VMEM, VMEM],
        [
            pltpu.VMEM((rows, 2 * HDIM), BF16),
            pltpu.VMEM((HDIM + 16, rows), F32),
            pltpu.VMEM((8, rows), F32),
        ],
        pl.CostEstimate(flops=10**10, bytes_accessed=5 * 10**6, transcendentals=12 * 10**6),
    )(received, prefix_keys, prefix_values)
    back = exchange(prefix)
    copies = call(merge_kernel, [((owners, requests, width), BF16)], [VMEM] * 4)(
        back, dest, suffix_out, suffix_lse
    )
    attention = lax.all_to_all(copies, "pfx", split_axis=0, concat_axis=0, tiled=True)
    attention = attention.reshape(owners * requests, width)
    columns = out_weight.shape[1]
    half = owners * requests // 2
    mine, other = call(
        project_kernel,
        [((half, columns), F32), ((half, columns), BF16)],
        [SMEM, VMEM, VMEM],
        (),
        pl.CostEstimate(flops=2 * 10**9, bytes_accessed=8 * 10**6, transcendentals=0),
    )(core, attention, out_weight)
    got = lax.ppermute(other, "tp", [(i, i ^ 1) for i in range(8)])
    block = half // 4
    own, *parts = call(
        pair_kernel, [((block, columns), F32)] + [((block, columns), BF16)] * 3, [SMEM, VMEM, VMEM]
    )(y, mine, got)
    arrived = [
        lax.ppermute(part, "tp", [(i, (i + 2 * k) % 8) for i in range(8)])
        for k, part in zip((1, 2, 3), parts)
    ]
    return call(sum_kernel, [((block, columns), BF16)], [VMEM] * 4)(own, *arrived)


def solution(mesh):
    placed = (
        P("pfx", "tp"),
        P("pfx"),
        P(),
        P("pfx"),
        P("pfx", "tp"),
        P("pfx", "tp"),
        P("pfx", None, "tp"),
        P("pfx", None, "tp"),
        P("tp", "pfx"),
    )
    return jax.shard_map(
        on_device, mesh=mesh, in_specs=placed, out_specs=P("tp", "pfx"), check_vma=False
    )
```

```python
import functools

import jax
import jax.numpy as jnp
from jax import lax
from jax.experimental import pallas as pl
from jax.experimental.pallas import tpu as pltpu
from jax.sharding import PartitionSpec as P

HDIM = 128
SLOTS = 8
CAP = 6
LOG2E = 1.4426950408889634
LN2 = 0.6931471805599453
F32 = jnp.float32
BF16 = jnp.bfloat16
VMEM = pl.BlockSpec(memory_space=pltpu.VMEM)
SMEM = pl.BlockSpec(memory_space=pltpu.SMEM)
HBM = pl.BlockSpec(memory_space=pltpu.HBM)
NT = (((1,), (1,)), ((), ()))


def iota(shape, dim):
    return lax.broadcasted_iota(jnp.int32, shape, dim)


def one_hot(condition):
    return jnp.where(condition, 1.0, 0.0).astype(BF16)


def dest_rows(route_ref, place_ref, count_ref, add):
    for owner in range(place_ref.shape[0]):
        count_ref[owner] = 0
    for r in range(route_ref.shape[0]):
        owner = place_ref[route_ref[r]]
        rank = count_ref[owner]
        count_ref[owner] = rank + 1
        add(r, owner * SLOTS + rank)


def pack_kernel(route_in, place_in, q_in, out_ref, route_ref, place_ref, q_ref, count_ref, sems):
    rows = q_ref.shape[0]
    pairs = [(route_in, route_ref), (place_in, place_ref), (q_in, q_ref)]
    loads = [pltpu.make_async_copy(a, b, sems.at[i]) for i, (a, b) in enumerate(pairs)]
    for load in loads:
        load.start()
    for load in loads[:2]:
        load.wait()
    lane = iota((SLOTS, 128), 1)
    dest = [jnp.full((SLOTS, 128), -1, jnp.int32)]

    def add(r, row):
        dest[0] = jnp.where(lane == r, row, dest[0])

    dest_rows(route_ref, place_ref, count_ref, add)
    pick = one_hot(iota((out_ref.shape[0], rows), 0) == dest[0][:1, :rows])
    loads[2].wait()
    rows_all = out_ref.shape[0]
    row, other = iota((rows_all, rows_all), 0), iota((rows_all, rows_all), 1)
    gather = one_hot((row % SLOTS == CAP) & (row // SLOTS == other // SLOTS))
    ones = jnp.ones((rows, 128), BF16)
    taken = jnp.dot(pick, ones, preferred_element_type=F32).astype(BF16)
    counts = jnp.dot(gather, taken, preferred_element_type=F32)
    out = jnp.dot(pick, q_ref[...], preferred_element_type=F32)
    out_ref[:, :128] = (out[:, :128] + counts).astype(BF16)
    out_ref[:, 128:] = out[:, 128:].astype(BF16)


def suffix_kernel(
    route_ref,
    place_ref,
    len_ref,
    q_ref,
    k_ref,
    v_ref,
    out_ref,
    lse_ref,
    dest_ref,
    count_ref,
):
    requests, cache, depth = k_ref.shape
    heads = q_ref.shape[1] // depth
    batch = 16
    dest = [jnp.zeros((requests, 128), jnp.int32)]
    row = iota((requests, 128), 0)

    def add(r, place):
        dest[0] = jnp.where(row == r, place, dest[0])

    dest_rows(route_ref, place_ref, count_ref, add)
    dest_ref[...] = dest[0]
    for b in range(requests // batch):
        first = b * batch
        sl = slice(first, first + batch)
        q = jnp.concatenate([q_ref[sl, h * depth : (h + 1) * depth] for h in range(heads)], axis=0)
        own = iota((batch, 128), 0)
        live = jnp.zeros((batch, 128), jnp.int32)
        for r in range(batch):
            live = jnp.where(own == r, len_ref[first + r], live)
        keys = k_ref[sl].reshape(batch * cache, depth)
        values = v_ref[sl].reshape(batch * cache, depth)
        scores = lax.dot_general(q, keys, NT, preferred_element_type=F32)
        column = iota((batch, batch * cache), 1)
        start = iota((batch, batch * cache), 0) * cache
        inside = (column >= start) & (column < start + live[:, :1])
        bias = jnp.where(inside, 0.0, -jnp.inf)
        scores = scores * (depth**-0.5 * LOG2E) + jnp.concatenate([bias] * heads, axis=0)
        top = jnp.max(scores, axis=1, keepdims=True)
        weights = jnp.exp2(scores - top).astype(BF16)
        both = jnp.dot(
            weights,
            jnp.concatenate([values, jnp.ones_like(values)], axis=1),
            preferred_element_type=F32,
        )
        total = both[:, depth:]
        out = both[:, :depth] / total
        lse = top * LN2 + jnp.log(total)
        for h in range(heads):
            part = slice(h * batch, (h + 1) * batch)
            out_ref[sl, h * depth : (h + 1) * depth] = out[part]
            lse_ref[sl, h * depth : (h + 1) * depth] = lse[part]


KEYS = 4096
GROUP = 32


def prefix_kernel(recv_ref, k_in, v_in, out_ref, k_ref, v_ref, q_ref, acc_ref, top_ref, sems):
    depth = k_ref.shape[1]
    buffer_rows, width = recv_ref.shape
    heads = width // depth
    cols = heads * GROUP
    items = buffer_rows // SLOTS * CAP
    blocks = items // GROUP
    steps = k_ref.shape[0] // KEYS
    loads = []
    for i in range(steps):
        sl = pl.ds(i * KEYS, KEYS)
        loads.append(pltpu.make_async_copy(k_in.at[sl, :], k_ref.at[sl, :], sems.at[0, i]))
        loads.append(pltpu.make_async_copy(v_in.at[sl, :], v_ref.at[sl, :], sems.at[1, i]))
    for load in loads:
        load.start()

    square = (buffer_rows, buffer_rows)
    row, other = iota(square, 0), iota(square, 1)
    counts = jnp.dot(
        one_hot(other == row // SLOTS * SLOTS + CAP),
        recv_ref[:, :buffer_rows],
        preferred_element_type=F32,
    )
    live = row % SLOTS < counts.astype(jnp.int32)
    live_bits = one_hot(live)
    place_down = jnp.dot(one_hot(other < row), live_bits, preferred_element_type=F32)
    place_down = place_down.astype(jnp.int32)
    live_across = jnp.where(live, 1.0, 0.0).T
    place_across = jnp.dot(
        live_across.astype(BF16), one_hot(row < other), preferred_element_type=F32
    ).astype(jnp.int32)
    used = jnp.sum(jnp.where(live[:, :1], 1.0, 0.0)).astype(jnp.int32)
    active = (used + GROUP - 1) // GROUP
    short = (items, buffer_rows)
    pick = one_hot((place_across[:items] == iota(short, 0)) & (live_across[:items] > 0.5))

    scale = depth**-0.5 * LOG2E
    for h in range(heads):
        q = jnp.dot(
            pick, recv_ref[:, h * depth : (h + 1) * depth], preferred_element_type=F32
        )
        q = q * scale
        high = q.astype(BF16)
        low = (q - high.astype(F32)).astype(BF16)
        for b in range(blocks):
            to = slice(b * cols + h * GROUP, b * cols + (h + 1) * GROUP)
            of = slice(b * GROUP, (b + 1) * GROUP)
            q_ref[to, :depth] = high[of]
            q_ref[to, depth:] = low[of]

    def scores_of(i, c):
        keys = k_ref[pl.ds(i * KEYS, KEYS), :]
        return lax.dot_general(
            jnp.concatenate([keys, keys], axis=1),
            q_ref[pl.ds(c * cols, cols), :],
            NT,
            preferred_element_type=F32,
        )

    def value_rows(i):
        values = v_ref[pl.ds(i * KEYS, KEYS), :]
        return jnp.concatenate([values.T, jnp.ones((16, KEYS), BF16)], axis=0)

    for c in range(blocks):
        start = jnp.where(c < active, 0.0, 1.0)
        acc_ref[:, c * cols : (c + 1) * cols] = jnp.full((acc_ref.shape[0], cols), start, F32)
    for i in range(steps):
        loads[2 * i].wait()
        loads[2 * i + 1].wait()
        turned = value_rows(i)
        for c in range(blocks):

            def add(c=c, i=i, turned=turned):
                weights = jnp.exp2(scores_of(i, c)).astype(BF16)
                acc_ref[:, c * cols : (c + 1) * cols] += jnp.dot(
                    turned, weights, preferred_element_type=F32
                )

            pl.when(c < active)(add)
    top_ref[...] = jnp.zeros_like(top_ref)
    total = acc_ref[depth : depth + 1, :]
    fine = (total > 2.0**-64) & (total < 2.0**100)

    @pl.when(jnp.min(jnp.where(fine, 1.0, 0.0)) < 0.5)
    def _():
        for c in range(blocks):
            sl = slice(c * cols, (c + 1) * cols)

            def find(i, top):
                return jnp.maximum(top, jnp.max(scores_of(i, c), axis=0, keepdims=True))

            top = lax.fori_loop(0, steps, find, jnp.full((1, cols), -jnp.inf, F32))
            top_ref[:, sl] = jnp.broadcast_to(top, (8, cols))
            acc_ref[:, sl] = jnp.zeros((acc_ref.shape[0], cols), F32)

            def again(i, carry):
                weights = jnp.exp2(scores_of(i, c) - top).astype(BF16)
                acc_ref[:, sl] += jnp.dot(value_rows(i), weights, preferred_element_type=F32)
                return carry

            lax.fori_loop(0, steps, again, 0)

    total = acc_ref[depth : depth + 1, :]
    inverse = 1.0 / total
    lse = top_ref[:1, :] * LN2 + jnp.log(total)
    high = lse.astype(BF16).astype(F32)
    middle = (lse - high).astype(BF16).astype(F32)
    low = lse - high - middle
    wide = iota((8, blocks * cols), 0)
    pieces = jnp.where(wide == 0, high, jnp.where(wide == 1, middle, low))
    tall = (buffer_rows, items)
    result_row = one_hot((place_down[:, :items] == iota(tall, 1)) & live[:, :items])
    gather = one_hot((row % SLOTS == CAP) & (row // SLOTS == other // SLOTS))
    lse_row = jnp.dot(gather, result_row, preferred_element_type=F32).astype(BF16)
    spread = jnp.concatenate([result_row, lse_row], axis=1)
    slot = jnp.dot(
        pick, (row % SLOTS).astype(F32).astype(BF16), preferred_element_type=F32
    ).astype(jnp.int32)
    offset = iota((items, depth), 1) - 3 * slot[:, :depth]
    four = depth // GROUP
    for h0 in range(0, heads, four):
        outs, threes = [], []
        for b in range(blocks):
            sl = slice(b * cols + h0 * GROUP, b * cols + (h0 + four) * GROUP)
            outs.append((acc_ref[:depth, sl] * inverse[:, sl]).T)
            threes.append(pieces[:, sl].T)
        for h in range(four):
            part = slice(h * GROUP, (h + 1) * GROUP)
            out = jnp.concatenate([x[part] for x in outs], axis=0)
            three = jnp.concatenate([x[part] for x in threes], axis=0)
            packed = jnp.where(
                offset == 0,
                three[:, 0:1],
                jnp.where(
                    offset == 1, three[:, 1:2], jnp.where(offset == 2, three[:, 2:3], 0.0)
                ),
            )
            both = jnp.concatenate([out.astype(BF16), packed.astype(BF16)], axis=0)
            out_ref[:, (h0 + h) * depth : (h0 + h + 1) * depth] = jnp.dot(
                spread, both, preferred_element_type=F32
            ).astype(BF16)


def merge_kernel(back_ref, dest_ref, suffix_ref, lse_ref, out_ref):
    copies, requests, width = out_ref.shape
    depth = HDIM
    dest = dest_ref[:, :1]
    column = iota((requests, back_ref.shape[0]), 1)
    pick_out = one_hot(column == dest)
    pick_lse = one_hot(column == dest // SLOTS * SLOTS + CAP)
    offset = iota((requests, depth), 1) - 3 * (dest % SLOTS)
    mine = (offset >= 0) & (offset < 3)
    for h in range(width // depth):
        sl = slice(h * depth, (h + 1) * depth)
        prefix = jnp.dot(pick_out, back_ref[:, sl], preferred_element_type=F32)
        pieces = jnp.dot(pick_lse, back_ref[:, sl], preferred_element_type=F32)
        prefix_lse = jnp.sum(jnp.where(mine, pieces, 0.0), axis=1, keepdims=True)
        suffix_lse = lse_ref[:, sl]
        top = jnp.maximum(prefix_lse, suffix_lse)
        prefix_part = jnp.exp(prefix_lse - top)
        suffix_part = jnp.exp(suffix_lse - top)
        merged = (prefix_part * prefix + suffix_part * suffix_ref[:, sl]) / (
            prefix_part + suffix_part
        )
        merged = merged.astype(BF16)
        for copy in range(copies):
            out_ref[copy, :, sl] = merged


TILE = 256


def project_kernel(core_ref, a_ref, w_ref, mine_ref, other_ref):
    core = core_ref[0]
    block = a_ref.shape[0] // 8
    half = 4 * block
    order = [(y, core) for y in range(4)] + [(y, 1 - core) for y in range(4)]
    a = jnp.concatenate(
        [a_ref[pl.ds(pl.multiple_of((2 * y + c) * block, block), block), :] for y, c in order],
        axis=0,
    )
    for n in range(w_ref.shape[1] // TILE):
        sl = slice(n * TILE, (n + 1) * TILE)
        out = jnp.dot(a, w_ref[:, sl], preferred_element_type=F32)
        mine_ref[:, sl] = out[:half]
        other_ref[:, sl] = out[half:].astype(BF16)


def pair_kernel(y_ref, mine_ref, got_ref, own_ref, one_ref, two_ref, three_ref):
    y = y_ref[0]
    block = own_ref.shape[0]

    def part(k):
        start = pl.multiple_of(lax.rem(y + k, 4) * block, block)
        return mine_ref[pl.ds(start, block), :] + got_ref[pl.ds(start, block), :].astype(F32)

    one_ref[...] = part(1).astype(BF16)
    two_ref[...] = part(2).astype(BF16)
    three_ref[...] = part(3).astype(BF16)
    own_ref[...] = part(0)


def sum_kernel(own_ref, one_ref, two_ref, three_ref, out_ref):
    out_ref[...] = (
        own_ref[...]
        + one_ref[...].astype(F32)
        + two_ref[...].astype(F32)
        + three_ref[...].astype(F32)
    ).astype(BF16)


def call(kernel, outs, specs, scratch=(), cost=None, mib=16):
    shapes = [jax.ShapeDtypeStruct(shape, dtype) for shape, dtype in outs]
    many = len(shapes) > 1
    return pl.pallas_call(
        kernel,
        out_shape=shapes if many else shapes[0],
        in_specs=specs,
        out_specs=[VMEM] * len(shapes) if many else VMEM,
        scratch_shapes=list(scratch),
        compiler_params=pltpu.CompilerParams(vmem_limit_bytes=mib * 2**20),
        cost_estimate=cost,
    )


def on_device(
    queries, route, place, suffix_len, prefix_keys, prefix_values, suffix_keys, suffix_values, out_weight
):
    requests, width = queries.shape
    owners = lax.axis_size("pfx")
    heads = width // HDIM
    buffer_rows = owners * SLOTS
    rows = owners * CAP * heads
    count = pltpu.SMEM((owners,), jnp.int32)
    tp = lax.axis_index("tp")
    core, y = (tp % 2).reshape(1), (tp // 2).reshape(1)

    def exchange(x):
        shape = x.shape
        x = x.reshape(owners, -1, shape[1])
        x = lax.all_to_all(x, "pfx", split_axis=0, concat_axis=0, tiled=True)
        return x.reshape(shape)

    packed = call(
        pack_kernel,
        [((buffer_rows, width), BF16)],
        [HBM, HBM, HBM],
        [
            pltpu.SMEM(route.shape, jnp.int32),
            pltpu.SMEM(place.shape, jnp.int32),
            pltpu.VMEM(queries.shape, BF16),
            count,
            pltpu.SemaphoreType.DMA((3,)),
        ],
        None,
        62,
    )(route, place, queries)
    received = exchange(packed)
    suffix_out, suffix_lse, dest = call(
        suffix_kernel,
        [((requests, width), F32), ((requests, width), F32), ((requests, 128), jnp.int32)],
        [SMEM, SMEM, SMEM, VMEM, VMEM, VMEM],
        [count],
        pl.CostEstimate(flops=2 * 10**9, bytes_accessed=5 * 10**6, transcendentals=2 * 10**6),
        32,
    )(route, place, suffix_len, queries, suffix_keys, suffix_values)
    prefix = call(
        prefix_kernel,
        [((buffer_rows, width), BF16)],
        [VMEM, HBM, HBM],
        [
            pltpu.VMEM(prefix_keys.shape, BF16),
            pltpu.VMEM(prefix_values.shape, BF16),
            pltpu.VMEM((rows, 2 * HDIM), BF16),
            pltpu.VMEM((HDIM + 16, rows), F32),
            pltpu.VMEM((8, rows), F32),
            pltpu.SemaphoreType.DMA((2, prefix_keys.shape[0] // KEYS)),
        ],
        pl.CostEstimate(flops=10**10, bytes_accessed=5 * 10**6, transcendentals=12 * 10**6),
        62,
    )(received, prefix_keys, prefix_values)
    back = exchange(prefix)
    copies = call(merge_kernel, [((owners, requests, width), BF16)], [VMEM] * 4)(
        back, dest, suffix_out, suffix_lse
    )
    attention = exchange(copies.reshape(owners * requests, width))
    columns = out_weight.shape[1]
    half = owners * requests // 2
    mine, other = call(
        project_kernel,
        [((half, columns), F32), ((half, columns), BF16)],
        [SMEM, VMEM, VMEM],
        (),
        pl.CostEstimate(flops=2 * 10**9, bytes_accessed=8 * 10**6, transcendentals=0),
        24,
    )(core, attention, out_weight)
    got = lax.ppermute(other, "tp", [(i, i ^ 1) for i in range(8)])
    block = half // 4
    own, *parts = call(
        pair_kernel, [((block, columns), F32)] + [((block, columns), BF16)] * 3, [SMEM, VMEM, VMEM]
    )(y, mine, got)
    arrived = [
        lax.ppermute(part, "tp", [(i, (i + 2 * k) % 8) for i in range(8)])
        for k, part in zip((1, 2, 3), parts)
    ]
    return call(sum_kernel, [((block, columns), BF16)], [VMEM] * 4)(own, *arrived)


def solution(mesh):
    placed = (
        P("pfx", "tp"),
        P("pfx"),
        P(),
        P("pfx"),
        P("pfx", "tp"),
        P("pfx", "tp"),
        P("pfx", None, "tp"),
        P("pfx", None, "tp"),
        P("tp", "pfx"),
    )
    return jax.shard_map(
        on_device, mesh=mesh, in_specs=placed, out_specs=P("tp", "pfx"), check_vma=False
    )
```

```python
import functools

import jax
import jax.numpy as jnp
from jax import lax
from jax.experimental import pallas as pl
from jax.experimental.pallas import tpu as pltpu
from jax.sharding import PartitionSpec as P

HDIM = 128
SLOTS = 8
EXTRA = 128
CAP = 6
LOG2E = 1.4426950408889634
LN2 = 0.6931471805599453
F32 = jnp.float32
BF16 = jnp.bfloat16
VMEM = pl.BlockSpec(memory_space=pltpu.VMEM)
SMEM = pl.BlockSpec(memory_space=pltpu.SMEM)
HBM = pl.BlockSpec(memory_space=pltpu.HBM)
NT = (((1,), (1,)), ((), ()))


def iota(shape, dim):
    return lax.broadcasted_iota(jnp.int32, shape, dim)


def one_hot(condition):
    return jnp.where(condition, 1.0, 0.0).astype(BF16)


def dest_rows(route_ref, place_ref, count_ref, add):
    for owner in range(place_ref.shape[0]):
        count_ref[owner] = 0
    for r in range(route_ref.shape[0]):
        owner = place_ref[route_ref[r]]
        rank = count_ref[owner]
        count_ref[owner] = rank + 1
        add(r, owner * SLOTS + rank)


def pack_kernel(route_in, place_in, q_in, out_ref, route_ref, place_ref, q_ref, count_ref, sems):
    rows = q_ref.shape[0]
    pairs = [(route_in, route_ref), (place_in, place_ref), (q_in, q_ref)]
    loads = [pltpu.make_async_copy(a, b, sems.at[i]) for i, (a, b) in enumerate(pairs)]
    for load in loads:
        load.start()
    for load in loads[:2]:
        load.wait()
    lane = iota((SLOTS, 128), 1)
    dest = [jnp.full((SLOTS, 128), -1, jnp.int32)]

    def add(r, row):
        dest[0] = jnp.where(lane == r, row, dest[0])

    dest_rows(route_ref, place_ref, count_ref, add)
    pick = one_hot(iota((out_ref.shape[0], rows), 0) == dest[0][:1, :rows])
    loads[2].wait()
    width = q_ref.shape[1]
    live = jnp.dot(pick, jnp.ones((rows, EXTRA), BF16), preferred_element_type=F32)
    out_ref[:, :width] = jnp.dot(pick, q_ref[...], preferred_element_type=F32).astype(BF16)
    out_ref[:, width:] = live.astype(BF16)


def suffix_kernel(
    route_ref,
    place_ref,
    len_ref,
    q_ref,
    k_ref,
    v_ref,
    out_ref,
    lse_ref,
    dest_ref,
    count_ref,
):
    requests, cache, depth = k_ref.shape
    heads = q_ref.shape[1] // depth
    batch = 16
    dest = [jnp.zeros((requests, 128), jnp.int32)]
    row = iota((requests, 128), 0)

    def add(r, place):
        dest[0] = jnp.where(row == r, place, dest[0])

    dest_rows(route_ref, place_ref, count_ref, add)
    dest_ref[...] = dest[0]
    for b in range(requests // batch):
        first = b * batch
        sl = slice(first, first + batch)
        q = jnp.concatenate([q_ref[sl, h * depth : (h + 1) * depth] for h in range(heads)], axis=0)
        own = iota((batch, 128), 0)
        live = jnp.zeros((batch, 128), jnp.int32)
        for r in range(batch):
            live = jnp.where(own == r, len_ref[first + r], live)
        keys = k_ref[sl].reshape(batch * cache, depth)
        values = v_ref[sl].reshape(batch * cache, depth)
        scores = lax.dot_general(q, keys, NT, preferred_element_type=F32)
        column = iota((batch, batch * cache), 1)
        start = iota((batch, batch * cache), 0) * cache
        inside = (column >= start) & (column < start + live[:, :1])
        bias = jnp.where(inside, 0.0, -jnp.inf)
        scores = scores * (depth**-0.5 * LOG2E) + jnp.concatenate([bias] * heads, axis=0)
        top = jnp.max(scores, axis=1, keepdims=True)
        weights = jnp.exp2(scores - top).astype(BF16)
        both = jnp.dot(
            weights,
            jnp.concatenate([values, jnp.ones_like(values)], axis=1),
            preferred_element_type=F32,
        )
        total = both[:, depth:]
        out = both[:, :depth] / total
        lse = top * LN2 + jnp.log(total)
        for h in range(heads):
            part = slice(h * batch, (h + 1) * batch)
            out_ref[sl, h * depth : (h + 1) * depth] = out[part]
            lse_ref[sl, h * depth : (h + 1) * depth] = lse[part]


CHUNKS = (1024, 3072, 4096)
GROUP = 32


def prefix_kernel(recv_ref, k_in, v_in, out_ref, k_ref, v_ref, q_ref, acc_ref, top_ref, sems):
    depth = k_ref.shape[1]
    buffer_rows = recv_ref.shape[0]
    width = recv_ref.shape[1] - EXTRA
    heads = width // depth
    cols = heads * GROUP
    items = buffer_rows // SLOTS * CAP
    blocks = items // GROUP
    steps = len(CHUNKS)
    spans = [slice(sum(CHUNKS[:i]), sum(CHUNKS[: i + 1])) for i in range(steps)]
    loads = [
        [
            pltpu.make_async_copy(k_in.at[sl, :], k_ref.at[sl, :], sems.at[0, i]),
            pltpu.make_async_copy(v_in.at[sl, :], v_ref.at[sl, :], sems.at[1, i]),
        ]
        for i, sl in enumerate(spans)
    ]
    for load in loads[0]:
        load.start()

    square = (buffer_rows, buffer_rows)
    row, other = iota(square, 0), iota(square, 1)
    bits = recv_ref[:, width:]
    place_down = jnp.dot(one_hot(other < row), bits, preferred_element_type=F32)
    place_across = lax.dot_general(
        bits, one_hot(row < other), (((0,), (0,)), ((), ())), preferred_element_type=F32
    )
    live_across = lax.dot_general(
        bits, one_hot(row == other), (((0,), (0,)), ((), ())), preferred_element_type=F32
    )
    live = bits.astype(F32) > 0.5
    place_down = jnp.where(live, place_down.astype(jnp.int32), -1)
    used = (jnp.max(place_down) + 1).astype(jnp.int32)
    active = (used + GROUP - 1) // GROUP
    short = (items, buffer_rows)
    pick = one_hot(
        (place_across[:items].astype(jnp.int32) == iota(short, 0)) & (live_across[:items] > 0.5)
    )

    scale = depth**-0.5 * LOG2E
    four = 4
    for h0 in range(0, heads, four):
        q = jnp.dot(
            pick, recv_ref[:, h0 * depth : (h0 + four) * depth], preferred_element_type=F32
        ).astype(BF16)
        for b in range(blocks):
            of = slice(b * GROUP, (b + 1) * GROUP)
            for h in range(four):
                start = b * cols + (h0 + h) * GROUP
                q_ref[start : start + GROUP, :] = q[of, h * depth : (h + 1) * depth]

    def scores_of(span, c):
        q = q_ref[c * cols : (c + 1) * cols, :]
        return lax.dot_general(k_ref[span, :], q, NT, preferred_element_type=F32) * scale

    def value_rows(span):
        values = v_ref[span, :]
        return jnp.concatenate([values.T, jnp.ones((16, values.shape[0]), BF16)], axis=0)

    for c in range(blocks):
        start = jnp.where(c < active, 0.0, 1.0)
        acc_ref[:, c * cols : (c + 1) * cols] = jnp.full((acc_ref.shape[0], cols), start, F32)

    def attend(block):
        for i, span in enumerate(spans):
            for load in loads[i]:
                load.wait()
            if i + 1 < steps:
                for load in loads[i + 1]:
                    load.start()
            turned = value_rows(span)
            for c in range(blocks):

                def body(c=c, span=span, turned=turned):
                    weights = jnp.exp2(scores_of(span, c)).astype(BF16)
                    acc_ref[:, c * cols : (c + 1) * cols] += jnp.dot(
                        turned, weights, preferred_element_type=F32
                    )

                block(c, body)

    @pl.when(active == blocks)
    def _():
        attend(lambda c, body: body())

    @pl.when(active < blocks)
    def _():
        attend(lambda c, body: pl.when(c < active)(body))

    top_ref[...] = jnp.zeros_like(top_ref)
    total = acc_ref[depth : depth + 1, :]
    fine = (total > 2.0**-64) & (total < 2.0**100)

    @pl.when(jnp.min(jnp.where(fine, 1.0, 0.0)) < 0.5)
    def _():
        for c in range(blocks):
            sl = slice(c * cols, (c + 1) * cols)

            def find(i, top):
                span = pl.ds(pl.multiple_of(i * CHUNKS[0], CHUNKS[0]), CHUNKS[0])
                return jnp.maximum(top, jnp.max(scores_of(span, c), axis=0, keepdims=True))

            again_steps = k_ref.shape[0] // CHUNKS[0]
            top = lax.fori_loop(0, again_steps, find, jnp.full((1, cols), -jnp.inf, F32))
            top_ref[:, sl] = jnp.broadcast_to(top, (8, cols))
            acc_ref[:, sl] = jnp.zeros((acc_ref.shape[0], cols), F32)

            def again(i, carry):
                span = pl.ds(pl.multiple_of(i * CHUNKS[0], CHUNKS[0]), CHUNKS[0])
                weights = jnp.exp2(scores_of(span, c) - top).astype(BF16)
                acc_ref[:, sl] += jnp.dot(value_rows(span), weights, preferred_element_type=F32)
                return carry

            lax.fori_loop(0, again_steps, again, 0)

    total = acc_ref[depth : depth + 1, :]
    inverse = 1.0 / total
    lse = top_ref[:1, :] * LN2 + jnp.log(total)
    high = lse.astype(BF16).astype(F32)
    middle = (lse - high).astype(BF16).astype(F32)
    low = lse - high - middle
    wide = iota((8, blocks * cols), 0)
    pieces = jnp.where(
        wide == 0, high, jnp.where(wide == 1, middle, jnp.where(wide == 2, low, 0.0))
    ).astype(BF16)
    tall = (buffer_rows, items)
    result_row = one_hot(place_down[:, :items] == iota(tall, 1))
    for h0 in range(0, heads, four):
        turned = []
        for b in range(blocks):
            sl = slice(b * cols + h0 * GROUP, b * cols + (h0 + four) * GROUP)
            turned.append((acc_ref[:depth, sl] * inverse[:, sl]).astype(BF16).T)
        out = jnp.concatenate(
            [
                jnp.concatenate([x[h * GROUP : (h + 1) * GROUP] for x in turned], axis=0)
                for h in range(four)
            ],
            axis=1,
        )
        out_ref[:, h0 * depth : (h0 + four) * depth] = jnp.dot(
            result_row, out, preferred_element_type=F32
        ).astype(BF16)
    spread = (EXTRA, cols)
    same_head = iota(spread, 0) // 8 == iota(spread, 1) // GROUP
    lse_out = jnp.zeros((buffer_rows, EXTRA), F32)
    for b in range(blocks):
        part = pieces[:, b * cols : (b + 1) * cols]
        by_head = jnp.where(same_head, jnp.concatenate([part] * heads, axis=0), 0.0).astype(BF16)
        item = b * GROUP + iota((buffer_rows, cols), 1) % GROUP
        to_row = one_hot(jnp.concatenate([place_down] * (cols // EXTRA), axis=1) == item)
        lse_out += lax.dot_general(to_row, by_head, NT, preferred_element_type=F32)
    out_ref[:, width:] = lse_out.astype(BF16)


def merge_kernel(back_ref, dest_ref, suffix_ref, lse_ref, out_ref):
    copies, requests, width = out_ref.shape
    part = width // 4
    column = iota((requests, back_ref.shape[0]), 1)
    pick = one_hot(column == dest_ref[:, :1])
    pieces = jnp.dot(pick, back_ref[:, width:], preferred_element_type=F32).astype(BF16)
    for n in range(4):
        sl = slice(n * part, (n + 1) * part)
        prefix = jnp.dot(pick, back_ref[:, sl], preferred_element_type=F32)
        head = n * (part // HDIM) + iota((EXTRA, part), 1) // HDIM
        prefix_lse = jnp.dot(
            pieces, one_hot(iota((EXTRA, part), 0) // 8 == head), preferred_element_type=F32
        )
        suffix_lse = lse_ref[:, sl]
        top = jnp.maximum(prefix_lse, suffix_lse)
        prefix_part = jnp.exp(prefix_lse - top)
        suffix_part = jnp.exp(suffix_lse - top)
        merged = (prefix_part * prefix + suffix_part * suffix_ref[:, sl]) / (
            prefix_part + suffix_part
        )
        merged = merged.astype(BF16)
        for copy in range(copies):
            out_ref[copy, :, sl] = merged


TILE = 256


def project_kernel(core_ref, a_ref, w_ref, mine_ref, other_ref):
    core = core_ref[0]
    block = a_ref.shape[0] // 8
    half = 4 * block
    order = [(y, core) for y in range(4)] + [(y, 1 - core) for y in range(4)]
    a = jnp.concatenate(
        [a_ref[pl.ds(pl.multiple_of((2 * y + c) * block, block), block), :] for y, c in order],
        axis=0,
    )
    for n in range(w_ref.shape[1] // TILE):
        sl = slice(n * TILE, (n + 1) * TILE)
        out = jnp.dot(a, w_ref[:, sl], preferred_element_type=F32)
        mine_ref[:, sl] = out[:half]
        other_ref[:, sl] = out[half:].astype(BF16)


def pair_kernel(y_ref, mine_ref, got_ref, own_ref, one_ref, two_ref, three_ref):
    y = y_ref[0]
    block = own_ref.shape[0]

    def part(k):
        start = pl.multiple_of(lax.rem(y + k, 4) * block, block)
        return mine_ref[pl.ds(start, block), :] + got_ref[pl.ds(start, block), :].astype(F32)

    one_ref[...] = part(1).astype(BF16)
    two_ref[...] = part(2).astype(BF16)
    three_ref[...] = part(3).astype(BF16)
    own_ref[...] = part(0)


def sum_kernel(own_ref, one_ref, two_ref, three_ref, out_ref):
    out_ref[...] = (
        own_ref[...]
        + one_ref[...].astype(F32)
        + two_ref[...].astype(F32)
        + three_ref[...].astype(F32)
    ).astype(BF16)


def call(kernel, outs, specs, scratch=(), cost=None, mib=16):
    shapes = [jax.ShapeDtypeStruct(shape, dtype) for shape, dtype in outs]
    many = len(shapes) > 1
    return pl.pallas_call(
        kernel,
        out_shape=shapes if many else shapes[0],
        in_specs=specs,
        out_specs=[VMEM] * len(shapes) if many else VMEM,
        scratch_shapes=list(scratch),
        compiler_params=pltpu.CompilerParams(vmem_limit_bytes=mib * 2**20),
        cost_estimate=cost,
    )


def on_device(
    queries, route, place, suffix_len, prefix_keys, prefix_values, suffix_keys, suffix_values, out_weight
):
    requests, width = queries.shape
    owners = lax.axis_size("pfx")
    heads = width // HDIM
    buffer_rows = owners * SLOTS
    rows = owners * CAP * heads
    count = pltpu.SMEM((owners,), jnp.int32)
    tp = lax.axis_index("tp")
    core, y = (tp % 2).reshape(1), (tp // 2).reshape(1)

    def exchange(x):
        shape = x.shape
        x = x.reshape(owners, -1, shape[1])
        x = lax.all_to_all(x, "pfx", split_axis=0, concat_axis=0, tiled=True)
        return x.reshape(shape)

    packed = call(
        pack_kernel,
        [((buffer_rows, width + EXTRA), BF16)],
        [HBM, HBM, HBM],
        [
            pltpu.SMEM(route.shape, jnp.int32),
            pltpu.SMEM(place.shape, jnp.int32),
            pltpu.VMEM(queries.shape, BF16),
            count,
            pltpu.SemaphoreType.DMA((3,)),
        ],
        None,
        62,
    )(route, place, queries)
    received = exchange(packed)
    suffix_out, suffix_lse, dest = call(
        suffix_kernel,
        [((requests, width), F32), ((requests, width), F32), ((requests, 128), jnp.int32)],
        [SMEM, SMEM, SMEM, VMEM, VMEM, VMEM],
        [count],
        pl.CostEstimate(flops=2 * 10**9, bytes_accessed=5 * 10**6, transcendentals=2 * 10**6),
        32,
    )(route, place, suffix_len, queries, suffix_keys, suffix_values)
    prefix = call(
        prefix_kernel,
        [((buffer_rows, width + EXTRA), BF16)],
        [VMEM, HBM, HBM],
        [
            pltpu.VMEM(prefix_keys.shape, BF16),
            pltpu.VMEM(prefix_values.shape, BF16),
            pltpu.VMEM((rows, HDIM), BF16),
            pltpu.VMEM((HDIM + 16, rows), F32),
            pltpu.VMEM((8, rows), F32),
            pltpu.SemaphoreType.DMA((2, len(CHUNKS))),
        ],
        pl.CostEstimate(flops=10**10, bytes_accessed=5 * 10**6, transcendentals=12 * 10**6),
        62,
    )(received, prefix_keys, prefix_values)
    back = exchange(prefix)
    copies = call(merge_kernel, [((owners, requests, width), BF16)], [VMEM] * 4)(
        back, dest, suffix_out, suffix_lse
    )
    attention = exchange(copies.reshape(owners * requests, width))
    columns = out_weight.shape[1]
    half = owners * requests // 2
    mine, other = call(
        project_kernel,
        [((half, columns), F32), ((half, columns), BF16)],
        [SMEM, VMEM, VMEM],
        (),
        pl.CostEstimate(flops=2 * 10**9, bytes_accessed=8 * 10**6, transcendentals=0),
        24,
    )(core, attention, out_weight)
    got = lax.ppermute(other, "tp", [(i, i ^ 1) for i in range(8)])
    block = half // 4
    own, *parts = call(
        pair_kernel, [((block, columns), F32)] + [((block, columns), BF16)] * 3, [SMEM, VMEM, VMEM]
    )(y, mine, got)
    arrived = [
        lax.ppermute(part, "tp", [(i, (i + 2 * k) % 8) for i in range(8)])
        for k, part in ((2, parts[1]), (1, parts[0]), (3, parts[2]))
    ]
    return call(sum_kernel, [((block, columns), BF16)], [VMEM] * 4)(own, *arrived)


def solution(mesh):
    placed = (
        P("pfx", "tp"),
        P("pfx"),
        P(),
        P("pfx"),
        P("pfx", "tp"),
        P("pfx", "tp"),
        P("pfx", None, "tp"),
        P("pfx", None, "tp"),
        P("tp", "pfx"),
    )
    return jax.shard_map(
        on_device, mesh=mesh, in_specs=placed, out_specs=P("tp", "pfx"), check_vma=False
    )
```

```python
import functools

import jax
import jax.numpy as jnp
from jax import lax
from jax.experimental import pallas as pl
from jax.experimental.pallas import tpu as pltpu
from jax.sharding import PartitionSpec as P

HDIM = 128
SLOTS = 8
EXTRA = 128
CAP = 6
LOG2E = 1.4426950408889634
LN2 = 0.6931471805599453
F32 = jnp.float32
BF16 = jnp.bfloat16
VMEM = pl.BlockSpec(memory_space=pltpu.VMEM)
SMEM = pl.BlockSpec(memory_space=pltpu.SMEM)
HBM = pl.BlockSpec(memory_space=pltpu.HBM)
NT = (((1,), (1,)), ((), ()))


def iota(shape, dim):
    return lax.broadcasted_iota(jnp.int32, shape, dim)


def one_hot(condition):
    return jnp.where(condition, 1.0, 0.0).astype(BF16)


def dest_rows(route_ref, place_ref, count_ref, add):
    for owner in range(place_ref.shape[0]):
        count_ref[owner] = 0
    for r in range(route_ref.shape[0]):
        owner = place_ref[route_ref[r]]
        rank = count_ref[owner]
        count_ref[owner] = rank + 1
        add(r, owner * SLOTS + rank)


def pack_kernel(route_in, place_in, q_in, out_ref, route_ref, place_ref, q_ref, count_ref, sems):
    rows = q_ref.shape[0]
    pairs = [(route_in, route_ref), (place_in, place_ref), (q_in, q_ref)]
    loads = [pltpu.make_async_copy(a, b, sems.at[i]) for i, (a, b) in enumerate(pairs)]
    for load in loads:
        load.start()
    for load in loads[:2]:
        load.wait()
    lane = iota((SLOTS, 128), 1)
    dest = [jnp.full((SLOTS, 128), -1, jnp.int32)]

    def add(r, row):
        dest[0] = jnp.where(lane == r, row, dest[0])

    dest_rows(route_ref, place_ref, count_ref, add)
    buffer_rows, wide = out_ref.shape[0], SLOTS * rows
    place = jnp.concatenate([dest[0][:1, :rows]] * SLOTS, axis=1)
    row, lane = iota((buffer_rows, wide), 0), iota((buffer_rows, wide), 1)
    owner = row // SLOTS * SLOTS
    fits = row % SLOTS == lane // rows
    count = jnp.dot(
        one_hot(dest[0][:1, :rows] // SLOTS * SLOTS == owner[:, :rows]),
        jnp.ones((rows, EXTRA), BF16),
        preferred_element_type=F32,
    )
    out_ref[:, CAP * 2 * HDIM :] = count.astype(BF16)
    loads[2].wait()
    stacked = by_half(q_ref)
    picks = [one_hot(fits & (place == owner + k)) for k in range(CAP)]
    out = jnp.dot(jnp.concatenate(picks, axis=0), stacked, preferred_element_type=F32)
    for k in range(CAP):
        out_ref[:, k * 2 * HDIM : (k + 1) * 2 * HDIM] = out[
            k * buffer_rows : (k + 1) * buffer_rows
        ].astype(BF16)


def by_half(ref):
    parts = []
    for sub in range(SLOTS):
        low, high = sub * HDIM, (SLOTS + sub) * HDIM
        parts.append(
            jnp.concatenate([ref[:, low : low + HDIM], ref[:, high : high + HDIM]], axis=1)
        )
    return jnp.concatenate(parts, axis=0)


def by_slot(ref):
    return jnp.concatenate(
        [ref[:, k * 2 * HDIM : (k + 1) * 2 * HDIM] for k in range(CAP)], axis=0
    )


def suffix_kernel(
    route_ref,
    place_ref,
    len_ref,
    q_ref,
    k_ref,
    v_ref,
    out_ref,
    lse_ref,
    dest_ref,
    count_ref,
):
    requests, cache, depth = k_ref.shape
    heads = q_ref.shape[1] // depth
    batch = 16
    dest = [jnp.zeros((requests, 128), jnp.int32)]
    row = iota((requests, 128), 0)

    def add(r, place):
        dest[0] = jnp.where(row == r, place, dest[0])

    dest_rows(route_ref, place_ref, count_ref, add)
    dest_ref[...] = dest[0]
    for b in range(requests // batch):
        first = b * batch
        sl = slice(first, first + batch)
        q = jnp.concatenate([q_ref[sl, h * depth : (h + 1) * depth] for h in range(heads)], axis=0)
        own = iota((batch, 128), 0)
        live = jnp.zeros((batch, 128), jnp.int32)
        for r in range(batch):
            live = jnp.where(own == r, len_ref[first + r], live)
        keys = k_ref[sl].reshape(batch * cache, depth)
        values = v_ref[sl].reshape(batch * cache, depth)
        scores = lax.dot_general(q, keys, NT, preferred_element_type=F32)
        column = iota((batch, batch * cache), 1)
        start = iota((batch, batch * cache), 0) * cache
        inside = (column >= start) & (column < start + live[:, :1])
        bias = jnp.where(inside, 0.0, -jnp.inf)
        scores = scores * (depth**-0.5 * LOG2E) + jnp.concatenate([bias] * heads, axis=0)
        top = jnp.max(scores, axis=1, keepdims=True)
        weights = jnp.exp2(scores - top).astype(BF16)
        both = jnp.dot(
            weights,
            jnp.concatenate([values, jnp.ones_like(values)], axis=1),
            preferred_element_type=F32,
        )
        total = both[:, depth:]
        out = both[:, :depth] / total
        lse = top * LN2 + jnp.log(total)
        for h in range(heads):
            part = slice(h * batch, (h + 1) * batch)
            out_ref[sl, h * depth : (h + 1) * depth] = out[part]
            lse_ref[sl, h * depth : (h + 1) * depth] = lse[part]


CHUNKS = (1024, 3072, 4096)
GROUP = 32


def prefix_kernel(recv_ref, k_in, v_in, out_ref, k_ref, v_ref, q_ref, acc_ref, top_ref, sems):
    depth = k_ref.shape[1]
    buffer_rows = recv_ref.shape[0]
    width = CAP * 2 * depth
    heads = 2 * SLOTS
    cols = heads * GROUP
    items = buffer_rows // SLOTS * CAP
    blocks = items // GROUP
    steps = len(CHUNKS)
    spans = [slice(sum(CHUNKS[:i]), sum(CHUNKS[: i + 1])) for i in range(steps)]
    loads = [
        [
            pltpu.make_async_copy(k_in.at[sl, :], k_ref.at[sl, :], sems.at[0, i]),
            pltpu.make_async_copy(v_in.at[sl, :], v_ref.at[sl, :], sems.at[1, i]),
        ]
        for i, sl in enumerate(spans)
    ]
    for load in loads[0]:
        load.start()

    square = (buffer_rows, buffer_rows)
    row, other = iota(square, 0), iota(square, 1)
    number = recv_ref[:, width:]
    first = (other % SLOTS == 0) & (other // SLOTS < row // SLOTS)
    first_turned = (row % SLOTS == 0) & (row // SLOTS < other // SLOTS)
    turn = (((0,), (0,)), ((), ()))
    base_down = jnp.dot(one_hot(first), number, preferred_element_type=F32)
    base_across = lax.dot_general(number, one_hot(first_turned), turn, preferred_element_type=F32)
    number_across = lax.dot_general(number, one_hot(row == other), turn, preferred_element_type=F32)
    number_down = number.astype(F32)
    used = jnp.max(base_down + number_down).astype(jnp.int32)
    active = jnp.minimum((used + GROUP - 1) // GROUP, blocks)
    place_down = [
        jnp.where(number_down > k, base_down + k, -1.0).astype(jnp.int32) for k in range(CAP)
    ]
    place_across = jnp.concatenate(
        [
            jnp.where(number_across[:1] > k, base_across[:1] + k, -1.0).astype(jnp.int32)
            for k in range(CAP)
        ],
        axis=1,
    )

    scale = depth**-0.5 * LOG2E
    received = by_slot(recv_ref)
    shape = (items, CAP * buffer_rows)
    found = place_across == iota(shape, 0)
    picks = [one_hot(found & (iota(shape, 1) % SLOTS == sub)) for sub in range(SLOTS)]
    q = jnp.dot(jnp.concatenate(picks, axis=0), received, preferred_element_type=F32).astype(BF16)
    for sub in range(SLOTS):
        for b in range(blocks):
            of = slice(sub * items + b * GROUP, sub * items + (b + 1) * GROUP)
            for half in range(2):
                start = b * cols + (half * SLOTS + sub) * GROUP
                q_ref[start : start + GROUP, :] = q[of, half * depth : (half + 1) * depth]

    def scores_of(span, c):
        q = q_ref[c * cols : (c + 1) * cols, :]
        return lax.dot_general(k_ref[span, :], q, NT, preferred_element_type=F32) * scale

    def value_rows(span):
        values = v_ref[span, :]
        return jnp.concatenate([values.T, jnp.ones((16, values.shape[0]), BF16)], axis=0)

    for c in range(blocks):
        start = jnp.where(c < active, 0.0, 1.0)
        acc_ref[:, c * cols : (c + 1) * cols] = jnp.full((acc_ref.shape[0], cols), start, F32)

    def attend(block):
        for i, span in enumerate(spans):
            for load in loads[i]:
                load.wait()
            if i + 1 < steps:
                for load in loads[i + 1]:
                    load.start()
            turned = value_rows(span)
            for c in range(blocks):

                def body(c=c, span=span, turned=turned):
                    weights = jnp.exp2(scores_of(span, c)).astype(BF16)
                    acc_ref[:, c * cols : (c + 1) * cols] += jnp.dot(
                        turned, weights, preferred_element_type=F32
                    )

                block(c, body)

    @pl.when(active == blocks)
    def _():
        attend(lambda c, body: body())

    @pl.when(active < blocks)
    def _():
        attend(lambda c, body: pl.when(c < active)(body))

    top_ref[...] = jnp.zeros_like(top_ref)
    total = acc_ref[depth : depth + 1, :]
    fine = (total > 2.0**-64) & (total < 2.0**100)

    @pl.when(jnp.min(jnp.where(fine, 1.0, 0.0)) < 0.5)
    def _():
        for c in range(blocks):
            sl = slice(c * cols, (c + 1) * cols)

            def find(i, top):
                span = pl.ds(pl.multiple_of(i * CHUNKS[0], CHUNKS[0]), CHUNKS[0])
                return jnp.maximum(top, jnp.max(scores_of(span, c), axis=0, keepdims=True))

            again_steps = k_ref.shape[0] // CHUNKS[0]
            top = lax.fori_loop(0, again_steps, find, jnp.full((1, cols), -jnp.inf, F32))
            top_ref[:, sl] = jnp.broadcast_to(top, (8, cols))
            acc_ref[:, sl] = jnp.zeros((acc_ref.shape[0], cols), F32)

            def again(i, carry):
                span = pl.ds(pl.multiple_of(i * CHUNKS[0], CHUNKS[0]), CHUNKS[0])
                weights = jnp.exp2(scores_of(span, c) - top).astype(BF16)
                acc_ref[:, sl] += jnp.dot(value_rows(span), weights, preferred_element_type=F32)
                return carry

            lax.fori_loop(0, again_steps, again, 0)

    total = acc_ref[depth : depth + 1, :]
    inverse = 1.0 / total
    lse = top_ref[:1, :] * LN2 + jnp.log(total)
    high = lse.astype(BF16).astype(F32)
    middle = (lse - high).astype(BF16).astype(F32)
    low = lse - high - middle
    wide = iota((8, blocks * cols), 0)
    pieces = jnp.where(
        wide == 0, high, jnp.where(wide == 1, middle, jnp.where(wide == 2, low, 0.0))
    ).astype(BF16)
    four = depth // GROUP
    outs = []
    for h0 in range(0, heads, four):
        turned = []
        for b in range(blocks):
            sl = slice(b * cols + h0 * GROUP, b * cols + (h0 + four) * GROUP)
            turned.append((acc_ref[:depth, sl] * inverse[:, sl]).astype(BF16).T)
        for h in range(four):
            outs.append(
                jnp.concatenate([x[h * GROUP : (h + 1) * GROUP] for x in turned], axis=0)
            )
    results = jnp.concatenate(
        [
            jnp.concatenate([outs[sub], outs[SLOTS + sub]], axis=1)
            for sub in range(SLOTS)
        ],
        axis=0,
    )
    shape = (buffer_rows, SLOTS * items)
    same = iota(shape, 0) % SLOTS == iota(shape, 1) // items
    item = iota(shape, 1) % items
    picks = [
        one_hot(same & (jnp.concatenate([place] * (shape[1] // EXTRA), axis=1) == item))
        for place in place_down
    ]
    out = jnp.dot(jnp.concatenate(picks, axis=0), results, preferred_element_type=F32)
    for k in range(CAP):
        out_ref[:, k * 2 * depth : (k + 1) * 2 * depth] = out[
            k * buffer_rows : (k + 1) * buffer_rows
        ].astype(BF16)
    spread = (EXTRA, cols)
    same_head = iota(spread, 0) // 8 == iota(spread, 1) // GROUP
    to_item = one_hot(iota((GROUP, cols), 1) % GROUP == iota((GROUP, cols), 0))
    listed = []
    for b in range(blocks):
        part = pieces[:, b * cols : (b + 1) * cols]
        by_head = jnp.where(same_head, jnp.concatenate([part] * heads, axis=0), 0.0).astype(BF16)
        listed.append(lax.dot_general(to_item, by_head, NT, preferred_element_type=F32))
    listed = jnp.concatenate(listed, axis=0).astype(BF16)
    own = row % SLOTS == other // 8 % SLOTS
    to_row = [one_hot(place[:, :items] == iota((buffer_rows, items), 1)) for place in place_down]
    rows_of = jnp.dot(jnp.concatenate(to_row, axis=0), listed, preferred_element_type=F32)
    ones, lanes = [], []
    for k in range(CAP):
        one = rows_of[k * buffer_rows : (k + 1) * buffer_rows]
        ones.append(jnp.where(own, one, 0.0).astype(BF16))
        to_lane = (other // 16 == k) & (other // 8 % 2 == row // 64) & (other % 8 == row % 8)
        lanes.append(one_hot(to_lane))
    tail = jnp.dot(
        jnp.concatenate(ones, axis=1), jnp.concatenate(lanes, axis=0), preferred_element_type=F32
    )
    out_ref[:, width:] = tail.astype(BF16)


def merge_kernel(back_ref, dest_ref, suffix_ref, lse_ref, out_ref):
    copies, requests, _ = out_ref.shape
    buffer_rows = back_ref.shape[0]
    dest = dest_ref[:, :1]
    returned = by_slot(back_ref)
    shape = (requests, CAP * buffer_rows)
    lane = iota(shape, 1)
    mine = lane % buffer_rows // SLOTS * SLOTS + lane // buffer_rows == dest
    short = (requests, buffer_rows)
    group = iota(short, 1) // SLOTS == dest // SLOTS
    slot = iota(short, 1) // 16 == dest % SLOTS
    wide = (EXTRA, 2 * HDIM)
    to_half = one_hot((iota(wide, 0) // 8 % 2 == iota(wide, 1) // HDIM) & (iota(wide, 0) % 8 < 3))
    picks = [one_hot(mine & (lane % SLOTS == sub)) for sub in range(SLOTS)]
    prefixes = jnp.dot(jnp.concatenate(picks, axis=0), returned, preferred_element_type=F32)
    picks = [one_hot(group & (iota(short, 1) % SLOTS == sub)) for sub in range(SLOTS)]
    pieces = jnp.dot(
        jnp.concatenate(picks, axis=0), back_ref[:, CAP * 2 * HDIM :], preferred_element_type=F32
    )
    pieces = jnp.where(jnp.concatenate([slot] * SLOTS, axis=0), pieces, 0.0).astype(BF16)
    lses = jnp.dot(pieces, to_half, preferred_element_type=F32)
    for sub in range(SLOTS):
        prefix = prefixes[sub * requests : (sub + 1) * requests]
        prefix_lse = lses[sub * requests : (sub + 1) * requests]
        for half in range(2):
            part = slice(half * HDIM, (half + 1) * HDIM)
            start = (half * SLOTS + sub) * HDIM
            sl = slice(start, start + HDIM)
            suffix_lse = lse_ref[:, sl]
            top = jnp.maximum(prefix_lse[:, part], suffix_lse)
            prefix_part = jnp.exp(prefix_lse[:, part] - top)
            suffix_part = jnp.exp(suffix_lse - top)
            merged = (prefix_part * prefix[:, part] + suffix_part * suffix_ref[:, sl]) / (
                prefix_part + suffix_part
            )
            merged = merged.astype(BF16)
            for copy in range(copies):
                out_ref[copy, :, sl] = merged


TILE = 256


def project_kernel(core_ref, a_ref, w_ref, mine_ref, other_ref):
    core = core_ref[0]
    block = a_ref.shape[0] // 8
    half = 4 * block
    order = [(y, core) for y in range(4)] + [(y, 1 - core) for y in range(4)]
    a = jnp.concatenate(
        [a_ref[pl.ds(pl.multiple_of((2 * y + c) * block, block), block), :] for y, c in order],
        axis=0,
    )
    for n in range(w_ref.shape[1] // TILE):
        sl = slice(n * TILE, (n + 1) * TILE)
        out = jnp.dot(a, w_ref[:, sl], preferred_element_type=F32)
        mine_ref[:, sl] = out[:half]
        other_ref[:, sl] = out[half:].astype(BF16)


def pair_kernel(y_ref, mine_ref, got_ref, own_ref, one_ref, two_ref, three_ref):
    y = y_ref[0]
    block = own_ref.shape[0]

    def part(k):
        start = pl.multiple_of(lax.rem(y + k, 4) * block, block)
        return mine_ref[pl.ds(start, block), :] + got_ref[pl.ds(start, block), :].astype(F32)

    one_ref[...] = part(1).astype(BF16)
    two_ref[...] = part(2).astype(BF16)
    three_ref[...] = part(3).astype(BF16)
    own_ref[...] = part(0)


def sum_kernel(own_ref, one_ref, two_ref, three_ref, out_ref):
    out_ref[...] = (
        own_ref[...]
        + one_ref[...].astype(F32)
        + two_ref[...].astype(F32)
        + three_ref[...].astype(F32)
    ).astype(BF16)


def call(kernel, outs, specs, scratch=(), cost=None, mib=16):
    shapes = [jax.ShapeDtypeStruct(shape, dtype) for shape, dtype in outs]
    many = len(shapes) > 1
    return pl.pallas_call(
        kernel,
        out_shape=shapes if many else shapes[0],
        in_specs=specs,
        out_specs=[VMEM] * len(shapes) if many else VMEM,
        scratch_shapes=list(scratch),
        compiler_params=pltpu.CompilerParams(vmem_limit_bytes=mib * 2**20),
        cost_estimate=cost,
    )


def on_device(
    queries, route, place, suffix_len, prefix_keys, prefix_values, suffix_keys, suffix_values, out_weight
):
    requests, width = queries.shape
    owners = lax.axis_size("pfx")
    heads = width // HDIM
    buffer_rows = owners * SLOTS
    rows = owners * CAP * heads
    count = pltpu.SMEM((owners,), jnp.int32)
    tp = lax.axis_index("tp")
    core, y = (tp % 2).reshape(1), (tp // 2).reshape(1)

    def exchange(x):
        shape = x.shape
        x = x.reshape(owners, -1, shape[1])
        x = lax.all_to_all(x, "pfx", split_axis=0, concat_axis=0, tiled=True)
        return x.reshape(shape)

    packed = call(
        pack_kernel,
        [((buffer_rows, CAP * 2 * HDIM + EXTRA), BF16)],
        [HBM, HBM, HBM],
        [
            pltpu.SMEM(route.shape, jnp.int32),
            pltpu.SMEM(place.shape, jnp.int32),
            pltpu.VMEM(queries.shape, BF16),
            count,
            pltpu.SemaphoreType.DMA((3,)),
        ],
        None,
        62,
    )(route, place, queries)
    received = exchange(packed)
    suffix_out, suffix_lse, dest = call(
        suffix_kernel,
        [((requests, width), F32), ((requests, width), F32), ((requests, 128), jnp.int32)],
        [SMEM, SMEM, SMEM, VMEM, VMEM, VMEM],
        [count],
        pl.CostEstimate(flops=2 * 10**9, bytes_accessed=5 * 10**6, transcendentals=2 * 10**6),
        32,
    )(route, place, suffix_len, queries, suffix_keys, suffix_values)
    prefix = call(
        prefix_kernel,
        [((buffer_rows, CAP * 2 * HDIM + EXTRA), BF16)],
        [VMEM, HBM, HBM],
        [
            pltpu.VMEM(prefix_keys.shape, BF16),
            pltpu.VMEM(prefix_values.shape, BF16),
            pltpu.VMEM((rows, HDIM), BF16),
            pltpu.VMEM((HDIM + 16, rows), F32),
            pltpu.VMEM((8, rows), F32),
            pltpu.SemaphoreType.DMA((2, len(CHUNKS))),
        ],
        pl.CostEstimate(flops=10**10, bytes_accessed=5 * 10**6, transcendentals=12 * 10**6),
        62,
    )(received, prefix_keys, prefix_values)
    back = exchange(prefix)
    copies = call(merge_kernel, [((owners, requests, width), BF16)], [VMEM] * 4)(
        back, dest, suffix_out, suffix_lse
    )
    attention = exchange(copies.reshape(owners * requests, width))
    columns = out_weight.shape[1]
    half = owners * requests // 2
    mine, other = call(
        project_kernel,
        [((half, columns), F32), ((half, columns), BF16)],
        [SMEM, VMEM, VMEM],
        (),
        pl.CostEstimate(flops=2 * 10**9, bytes_accessed=8 * 10**6, transcendentals=0),
        24,
    )(core, attention, out_weight)
    got = lax.ppermute(other, "tp", [(i, i ^ 1) for i in range(8)])
    block = half // 4
    own, *parts = call(
        pair_kernel, [((block, columns), F32)] + [((block, columns), BF16)] * 3, [SMEM, VMEM, VMEM]
    )(y, mine, got)
    arrived = [
        lax.ppermute(part, "tp", [(i, (i + 2 * k) % 8) for i in range(8)])
        for k, part in ((2, parts[1]), (1, parts[0]), (3, parts[2]))
    ]
    return call(sum_kernel, [((block, columns), BF16)], [VMEM] * 4)(own, *arrived)


def solution(mesh):
    placed = (
        P("pfx", "tp"),
        P("pfx"),
        P(),
        P("pfx"),
        P("pfx", "tp"),
        P("pfx", "tp"),
        P("pfx", None, "tp"),
        P("pfx", None, "tp"),
        P("tp", "pfx"),
    )
    return jax.shard_map(
        on_device, mesh=mesh, in_specs=placed, out_specs=P("tp", "pfx"), check_vma=False
    )
```

```python
import functools

import jax
import jax.numpy as jnp
from jax import lax
from jax.experimental import pallas as pl
from jax.experimental.pallas import tpu as pltpu
from jax.sharding import PartitionSpec as P

HDIM = 128
SLOTS = 8
EXTRA = 128
CAP = 6
LOG2E = 1.4426950408889634
LN2 = 0.6931471805599453
F32 = jnp.float32
BF16 = jnp.bfloat16
VMEM = pl.BlockSpec(memory_space=pltpu.VMEM)
SMEM = pl.BlockSpec(memory_space=pltpu.SMEM)
HBM = pl.BlockSpec(memory_space=pltpu.HBM)
NT = (((1,), (1,)), ((), ()))


def iota(shape, dim):
    return lax.broadcasted_iota(jnp.int32, shape, dim)


def one_hot(condition):
    return jnp.where(condition, 1.0, 0.0).astype(BF16)


def dest_rows(route_ref, place_ref, count_ref, add):
    for owner in range(place_ref.shape[0]):
        count_ref[owner] = 0
    for r in range(route_ref.shape[0]):
        owner = place_ref[route_ref[r]]
        rank = count_ref[owner]
        count_ref[owner] = rank + 1
        add(r, owner * SLOTS + rank)


def pack_kernel(route_in, place_in, q_in, out_ref, route_ref, place_ref, q_ref, count_ref, sems):
    rows = q_ref.shape[0]
    pairs = [(route_in, route_ref), (place_in, place_ref), (q_in, q_ref)]
    loads = [pltpu.make_async_copy(a, b, sems.at[i]) for i, (a, b) in enumerate(pairs)]
    for load in loads:
        load.start()
    for load in loads[:2]:
        load.wait()
    lane = iota((SLOTS, 128), 1)
    dest = [jnp.full((SLOTS, 128), -1, jnp.int32)]

    def add(r, row):
        dest[0] = jnp.where(lane == r, row, dest[0])

    dest_rows(route_ref, place_ref, count_ref, add)
    buffer_rows, wide = out_ref.shape[0], SLOTS * rows
    place = jnp.concatenate([dest[0][:1, :rows]] * SLOTS, axis=1)
    row, lane = iota((buffer_rows, wide), 0), iota((buffer_rows, wide), 1)
    owner = row // SLOTS * SLOTS
    fits = row % SLOTS == lane // rows
    count = jnp.dot(
        one_hot(dest[0][:1, :rows] // SLOTS * SLOTS == owner[:, :rows]),
        jnp.ones((rows, EXTRA), BF16),
        preferred_element_type=F32,
    )
    out_ref[:, CAP * 2 * HDIM :] = count.astype(BF16)
    loads[2].wait()
    stacked = by_half(q_ref)
    picks = [one_hot(fits & (place == owner + k)) for k in range(CAP)]
    out = jnp.dot(jnp.concatenate(picks, axis=0), stacked, preferred_element_type=F32)
    for k in range(CAP):
        out_ref[:, k * 2 * HDIM : (k + 1) * 2 * HDIM] = out[
            k * buffer_rows : (k + 1) * buffer_rows
        ].astype(BF16)


def by_half(ref):
    parts = []
    for sub in range(SLOTS):
        low, high = sub * HDIM, (SLOTS + sub) * HDIM
        parts.append(
            jnp.concatenate([ref[:, low : low + HDIM], ref[:, high : high + HDIM]], axis=1)
        )
    return jnp.concatenate(parts, axis=0)


def by_slot(ref):
    return jnp.concatenate(
        [ref[:, k * 2 * HDIM : (k + 1) * 2 * HDIM] for k in range(CAP)], axis=0
    )


def suffix_kernel(
    route_ref,
    place_ref,
    len_ref,
    q_ref,
    k_in,
    v_in,
    out_ref,
    lse_ref,
    dest_ref,
    k_ref,
    v_ref,
    count_ref,
    sems,
):
    requests, cache, depth = k_ref.shape
    heads = q_ref.shape[1] // depth
    batch = 16
    loads = []
    for b in range(requests // batch):
        sl = pl.ds(b * batch, batch)
        loads.append(pltpu.make_async_copy(k_in.at[sl], k_ref.at[sl], sems.at[0, b]))
        loads.append(pltpu.make_async_copy(v_in.at[sl], v_ref.at[sl], sems.at[1, b]))
    for load in loads:
        load.start()
    dest = [jnp.zeros((requests, 128), jnp.int32)]
    row = iota((requests, 128), 0)

    def add(r, place):
        dest[0] = jnp.where(row == r, place, dest[0])

    dest_rows(route_ref, place_ref, count_ref, add)
    dest_ref[...] = dest[0]
    for b in range(requests // batch):
        first = b * batch
        sl = slice(first, first + batch)
        q = jnp.concatenate([q_ref[sl, h * depth : (h + 1) * depth] for h in range(heads)], axis=0)
        own = iota((batch, 128), 0)
        live = jnp.zeros((batch, 128), jnp.int32)
        for r in range(batch):
            live = jnp.where(own == r, len_ref[first + r], live)
        loads[2 * b].wait()
        loads[2 * b + 1].wait()
        keys = k_ref[sl].reshape(batch * cache, depth)
        values = v_ref[sl].reshape(batch * cache, depth)
        scores = lax.dot_general(q, keys, NT, preferred_element_type=F32)
        column = iota((batch, batch * cache), 1)
        start = iota((batch, batch * cache), 0) * cache
        inside = (column >= start) & (column < start + live[:, :1])
        bias = jnp.where(inside, 0.0, -jnp.inf)
        scores = scores * (depth**-0.5 * LOG2E) + jnp.concatenate([bias] * heads, axis=0)
        top = jnp.max(scores, axis=1, keepdims=True)
        weights = jnp.exp2(scores - top).astype(BF16)
        both = jnp.dot(
            weights,
            jnp.concatenate([values, jnp.ones_like(values)], axis=1),
            preferred_element_type=F32,
        )
        total = both[:, depth:]
        out = both[:, :depth] / total
        lse = top * LN2 + jnp.log(total)
        for h in range(heads):
            part = slice(h * batch, (h + 1) * batch)
            out_ref[sl, h * depth : (h + 1) * depth] = out[part]
            lse_ref[sl, h * depth : (h + 1) * depth] = lse[part]


CHUNKS = (1024, 3072, 4096)
GROUP = 32


def prefix_kernel(recv_ref, k_in, v_in, out_ref, k_ref, v_ref, q_ref, acc_ref, top_ref, sems):
    depth = k_ref.shape[1]
    buffer_rows = recv_ref.shape[0]
    width = CAP * 2 * depth
    heads = 2 * SLOTS
    cols = heads * GROUP
    items = buffer_rows // SLOTS * CAP
    blocks = items // GROUP
    steps = len(CHUNKS)
    spans = [slice(sum(CHUNKS[:i]), sum(CHUNKS[: i + 1])) for i in range(steps)]
    loads = [
        [
            pltpu.make_async_copy(k_in.at[sl, :], k_ref.at[sl, :], sems.at[0, i]),
            pltpu.make_async_copy(v_in.at[sl, :], v_ref.at[sl, :], sems.at[1, i]),
        ]
        for i, sl in enumerate(spans)
    ]
    for load in loads[0]:
        load.start()

    square = (buffer_rows, buffer_rows)
    row, other = iota(square, 0), iota(square, 1)
    number = recv_ref[:, width:]
    first = (other % SLOTS == 0) & (other // SLOTS < row // SLOTS)
    first_turned = (row % SLOTS == 0) & (row // SLOTS < other // SLOTS)
    turn = (((0,), (0,)), ((), ()))
    base_down = jnp.dot(one_hot(first), number, preferred_element_type=F32)
    base_across = lax.dot_general(number, one_hot(first_turned), turn, preferred_element_type=F32)
    number_across = lax.dot_general(number, one_hot(row == other), turn, preferred_element_type=F32)
    number_down = number.astype(F32)
    used = jnp.max(base_down + number_down).astype(jnp.int32)
    active = jnp.minimum((used + GROUP - 1) // GROUP, blocks)
    place_down = [
        jnp.where(number_down > k, base_down + k, -1.0).astype(jnp.int32) for k in range(CAP)
    ]
    place_across = jnp.concatenate(
        [
            jnp.where(number_across[:1] > k, base_across[:1] + k, -1.0).astype(jnp.int32)
            for k in range(CAP)
        ],
        axis=1,
    )

    scale = depth**-0.5 * LOG2E
    received = by_slot(recv_ref)
    shape = (items, CAP * buffer_rows)
    found = place_across == iota(shape, 0)
    picks = [one_hot(found & (iota(shape, 1) % SLOTS == sub)) for sub in range(SLOTS)]
    q = jnp.dot(jnp.concatenate(picks, axis=0), received, preferred_element_type=F32).astype(BF16)
    for sub in range(SLOTS):
        for b in range(blocks):
            of = slice(sub * items + b * GROUP, sub * items + (b + 1) * GROUP)
            for half in range(2):
                start = b * cols + (half * SLOTS + sub) * GROUP
                q_ref[start : start + GROUP, :] = q[of, half * depth : (half + 1) * depth]

    def scores_of(span, c):
        q = q_ref[c * cols : (c + 1) * cols, :]
        return lax.dot_general(k_ref[span, :], q, NT, preferred_element_type=F32) * scale

    def value_rows(span):
        values = v_ref[span, :]
        return jnp.concatenate([values.T, jnp.ones((16, values.shape[0]), BF16)], axis=0)

    for c in range(blocks):
        start = jnp.where(c < active, 0.0, 1.0)
        acc_ref[:, c * cols : (c + 1) * cols] = jnp.full((acc_ref.shape[0], cols), start, F32)

    def attend(block):
        for i, span in enumerate(spans):
            for load in loads[i]:
                load.wait()
            if i + 1 < steps:
                for load in loads[i + 1]:
                    load.start()
            turned = value_rows(span)
            for c in range(blocks):

                def body(c=c, span=span, turned=turned):
                    weights = jnp.exp2(scores_of(span, c)).astype(BF16)
                    acc_ref[:, c * cols : (c + 1) * cols] += jnp.dot(
                        turned, weights, preferred_element_type=F32
                    )

                block(c, body)

    @pl.when(active == blocks)
    def _():
        attend(lambda c, body: body())

    @pl.when(active < blocks)
    def _():
        attend(lambda c, body: pl.when(c < active)(body))

    top_ref[...] = jnp.zeros_like(top_ref)
    total = acc_ref[depth : depth + 1, :]
    fine = (total > 2.0**-64) & (total < 2.0**100)

    @pl.when(jnp.min(jnp.where(fine, 1.0, 0.0)) < 0.5)
    def _():
        for c in range(blocks):
            sl = slice(c * cols, (c + 1) * cols)

            def find(i, top):
                span = pl.ds(pl.multiple_of(i * CHUNKS[0], CHUNKS[0]), CHUNKS[0])
                return jnp.maximum(top, jnp.max(scores_of(span, c), axis=0, keepdims=True))

            again_steps = k_ref.shape[0] // CHUNKS[0]
            top = lax.fori_loop(0, again_steps, find, jnp.full((1, cols), -jnp.inf, F32))
            top_ref[:, sl] = jnp.broadcast_to(top, (8, cols))
            acc_ref[:, sl] = jnp.zeros((acc_ref.shape[0], cols), F32)

            def again(i, carry):
                span = pl.ds(pl.multiple_of(i * CHUNKS[0], CHUNKS[0]), CHUNKS[0])
                weights = jnp.exp2(scores_of(span, c) - top).astype(BF16)
                acc_ref[:, sl] += jnp.dot(value_rows(span), weights, preferred_element_type=F32)
                return carry

            lax.fori_loop(0, again_steps, again, 0)

    total = acc_ref[depth : depth + 1, :]
    inverse = 1.0 / total
    lse = top_ref[:1, :] * LN2 + jnp.log(total)
    high = lse.astype(BF16).astype(F32)
    middle = (lse - high).astype(BF16).astype(F32)
    low = lse - high - middle
    wide = iota((8, blocks * cols), 0)
    pieces = jnp.where(
        wide == 0, high, jnp.where(wide == 1, middle, jnp.where(wide == 2, low, 0.0))
    ).astype(BF16)
    four = depth // GROUP
    outs = []
    for h0 in range(0, heads, four):
        turned = []
        for b in range(blocks):
            sl = slice(b * cols + h0 * GROUP, b * cols + (h0 + four) * GROUP)
            turned.append((acc_ref[:depth, sl] * inverse[:, sl]).astype(BF16).T)
        for h in range(four):
            outs.append(
                jnp.concatenate([x[h * GROUP : (h + 1) * GROUP] for x in turned], axis=0)
            )
    results = jnp.concatenate(
        [
            jnp.concatenate([outs[sub], outs[SLOTS + sub]], axis=1)
            for sub in range(SLOTS)
        ],
        axis=0,
    )
    shape = (buffer_rows, SLOTS * items)
    same = iota(shape, 0) % SLOTS == iota(shape, 1) // items
    item = iota(shape, 1) % items
    picks = [
        one_hot(same & (jnp.concatenate([place] * (shape[1] // EXTRA), axis=1) == item))
        for place in place_down
    ]
    out = jnp.dot(jnp.concatenate(picks, axis=0), results, preferred_element_type=F32)
    for k in range(CAP):
        out_ref[:, k * 2 * depth : (k + 1) * 2 * depth] = out[
            k * buffer_rows : (k + 1) * buffer_rows
        ].astype(BF16)
    spread = (EXTRA, cols)
    same_head = iota(spread, 0) // 8 == iota(spread, 1) // GROUP
    to_item = one_hot(iota((GROUP, cols), 1) % GROUP == iota((GROUP, cols), 0))
    listed = []
    for b in range(blocks):
        part = pieces[:, b * cols : (b + 1) * cols]
        by_head = jnp.where(same_head, jnp.concatenate([part] * heads, axis=0), 0.0).astype(BF16)
        listed.append(lax.dot_general(to_item, by_head, NT, preferred_element_type=F32))
    listed = jnp.concatenate(listed, axis=0).astype(BF16)
    own = row % SLOTS == other // 8 % SLOTS
    to_row = [one_hot(place[:, :items] == iota((buffer_rows, items), 1)) for place in place_down]
    rows_of = jnp.dot(jnp.concatenate(to_row, axis=0), listed, preferred_element_type=F32)
    ones, lanes = [], []
    for k in range(CAP):
        one = rows_of[k * buffer_rows : (k + 1) * buffer_rows]
        ones.append(jnp.where(own, one, 0.0).astype(BF16))
        to_lane = (other // 16 == k) & (other // 8 % 2 == row // 64) & (other % 8 == row % 8)
        lanes.append(one_hot(to_lane))
    tail = jnp.dot(
        jnp.concatenate(ones, axis=1), jnp.concatenate(lanes, axis=0), preferred_element_type=F32
    )
    out_ref[:, width:] = tail.astype(BF16)


def merge_kernel(back_ref, dest_ref, suffix_ref, lse_ref, out_ref):
    copies, requests, _ = out_ref.shape
    buffer_rows = back_ref.shape[0]
    dest = dest_ref[:, :1]
    returned = by_slot(back_ref)
    shape = (requests, CAP * buffer_rows)
    lane = iota(shape, 1)
    mine = lane % buffer_rows // SLOTS * SLOTS + lane // buffer_rows == dest
    short = (requests, buffer_rows)
    group = iota(short, 1) // SLOTS == dest // SLOTS
    slot = iota(short, 1) // 16 == dest % SLOTS
    wide = (EXTRA, 2 * HDIM)
    to_half = one_hot((iota(wide, 0) // 8 % 2 == iota(wide, 1) // HDIM) & (iota(wide, 0) % 8 < 3))
    picks = [one_hot(mine & (lane % SLOTS == sub)) for sub in range(SLOTS)]
    prefixes = jnp.dot(jnp.concatenate(picks, axis=0), returned, preferred_element_type=F32)
    picks = [one_hot(group & (iota(short, 1) % SLOTS == sub)) for sub in range(SLOTS)]
    pieces = jnp.dot(
        jnp.concatenate(picks, axis=0), back_ref[:, CAP * 2 * HDIM :], preferred_element_type=F32
    )
    pieces = jnp.where(jnp.concatenate([slot] * SLOTS, axis=0), pieces, 0.0).astype(BF16)
    lses = jnp.dot(pieces, to_half, preferred_element_type=F32)
    for sub in range(SLOTS):
        prefix = prefixes[sub * requests : (sub + 1) * requests]
        prefix_lse = lses[sub * requests : (sub + 1) * requests]
        for half in range(2):
            part = slice(half * HDIM, (half + 1) * HDIM)
            start = (half * SLOTS + sub) * HDIM
            sl = slice(start, start + HDIM)
            suffix_lse = lse_ref[:, sl]
            top = jnp.maximum(prefix_lse[:, part], suffix_lse)
            prefix_part = jnp.exp(prefix_lse[:, part] - top)
            suffix_part = jnp.exp(suffix_lse - top)
            merged = (prefix_part * prefix[:, part] + suffix_part * suffix_ref[:, sl]) / (
                prefix_part + suffix_part
            )
            merged = merged.astype(BF16)
            for copy in range(copies):
                out_ref[copy, :, sl] = merged


DEEP = 512
TILE = 256


def project_kernel(core_ref, a_ref, w_in, mine_ref, other_ref, w_ref, acc_ref, sems):
    steps = w_ref.shape[0] // DEEP
    loads = []
    for n in range(steps):
        sl = pl.ds(n * DEEP, DEEP)
        loads.append(pltpu.make_async_copy(w_in.at[sl, :], w_ref.at[sl, :], sems.at[n]))
        loads[n].start()
    core = core_ref[0]
    block = a_ref.shape[0] // 8
    half = 4 * block
    order = [(y, core) for y in range(4)] + [(y, 1 - core) for y in range(4)]
    a = jnp.concatenate(
        [a_ref[pl.ds(pl.multiple_of((2 * y + c) * block, block), block), :] for y, c in order],
        axis=0,
    )
    for n in range(steps):
        loads[n].wait()
        deep = slice(n * DEEP, (n + 1) * DEEP)
        for t in range(w_ref.shape[1] // TILE):
            sl = slice(t * TILE, (t + 1) * TILE)
            out = jnp.dot(a[:, deep], w_ref[deep, sl], preferred_element_type=F32)
            if n > 0:
                out += acc_ref[:, sl]
            if n + 1 < steps:
                acc_ref[:, sl] = out
            else:
                mine_ref[:, sl] = out[:half]
                other_ref[:, sl] = out[half:].astype(BF16)


def pair_kernel(y_ref, mine_ref, got_ref, own_ref, one_ref, two_ref, three_ref):
    y = y_ref[0]
    block = own_ref.shape[0]

    def part(k):
        start = pl.multiple_of(lax.rem(y + k, 4) * block, block)
        return mine_ref[pl.ds(start, block), :] + got_ref[pl.ds(start, block), :].astype(F32)

    one_ref[...] = part(1).astype(BF16)
    two_ref[...] = part(2).astype(BF16)
    three_ref[...] = part(3).astype(BF16)
    own_ref[...] = part(0)


def sum_kernel(own_ref, one_ref, two_ref, three_ref, out_ref):
    out_ref[...] = (
        own_ref[...]
        + one_ref[...].astype(F32)
        + two_ref[...].astype(F32)
        + three_ref[...].astype(F32)
    ).astype(BF16)


def in_hbm(array):
    return pltpu.with_memory_space_constraint(array, pltpu.HBM)


def call(kernel, outs, specs, scratch=(), cost=None, mib=16):
    shapes = [jax.ShapeDtypeStruct(shape, dtype) for shape, dtype in outs]
    many = len(shapes) > 1
    return pl.pallas_call(
        kernel,
        out_shape=shapes if many else shapes[0],
        in_specs=specs,
        out_specs=[VMEM] * len(shapes) if many else VMEM,
        scratch_shapes=list(scratch),
        compiler_params=pltpu.CompilerParams(vmem_limit_bytes=mib * 2**20),
        cost_estimate=cost,
    )


def on_device(
    queries, route, place, suffix_len, prefix_keys, prefix_values, suffix_keys, suffix_values, out_weight
):
    requests, width = queries.shape
    owners = lax.axis_size("pfx")
    heads = width // HDIM
    buffer_rows = owners * SLOTS
    rows = owners * CAP * heads
    count = pltpu.SMEM((owners,), jnp.int32)
    tp = lax.axis_index("tp")
    core, y = (tp % 2).reshape(1), (tp // 2).reshape(1)

    def exchange(x):
        shape = x.shape
        x = x.reshape(owners, -1, shape[1])
        x = lax.all_to_all(x, "pfx", split_axis=0, concat_axis=0, tiled=True)
        return x.reshape(shape)

    packed = call(
        pack_kernel,
        [((buffer_rows, CAP * 2 * HDIM + EXTRA), BF16)],
        [HBM, HBM, HBM],
        [
            pltpu.SMEM(route.shape, jnp.int32),
            pltpu.SMEM(place.shape, jnp.int32),
            pltpu.VMEM(queries.shape, BF16),
            count,
            pltpu.SemaphoreType.DMA((3,)),
        ],
        None,
        62,
    )(in_hbm(route), in_hbm(place), in_hbm(queries))
    received = exchange(packed)
    suffix_out, suffix_lse, dest = call(
        suffix_kernel,
        [((requests, width), F32), ((requests, width), F32), ((requests, 128), jnp.int32)],
        [SMEM, SMEM, SMEM, VMEM, HBM, HBM],
        [
            pltpu.VMEM(suffix_keys.shape, BF16),
            pltpu.VMEM(suffix_values.shape, BF16),
            count,
            pltpu.SemaphoreType.DMA((2, 2)),
        ],
        pl.CostEstimate(flops=2 * 10**9, bytes_accessed=5 * 10**6, transcendentals=2 * 10**6),
        32,
    )(route, place, suffix_len, queries, in_hbm(suffix_keys), in_hbm(suffix_values))
    prefix = call(
        prefix_kernel,
        [((buffer_rows, CAP * 2 * HDIM + EXTRA), BF16)],
        [VMEM, HBM, HBM],
        [
            pltpu.VMEM(prefix_keys.shape, BF16),
            pltpu.VMEM(prefix_values.shape, BF16),
            pltpu.VMEM((rows, HDIM), BF16),
            pltpu.VMEM((HDIM + 16, rows), F32),
            pltpu.VMEM((8, rows), F32),
            pltpu.SemaphoreType.DMA((2, len(CHUNKS))),
        ],
        pl.CostEstimate(flops=10**10, bytes_accessed=5 * 10**6, transcendentals=12 * 10**6),
        44,
    )(received, in_hbm(prefix_keys), in_hbm(prefix_values))
    back = exchange(prefix)
    copies = call(merge_kernel, [((owners, requests, width), BF16)], [VMEM] * 4)(
        back, dest, suffix_out, suffix_lse
    )
    attention = exchange(copies.reshape(owners * requests, width))
    columns = out_weight.shape[1]
    half = owners * requests // 2
    mine, other = call(
        project_kernel,
        [((half, columns), F32), ((half, columns), BF16)],
        [SMEM, VMEM, HBM],
        [
            pltpu.VMEM(out_weight.shape, BF16),
            pltpu.VMEM((2 * half, columns), F32),
            pltpu.SemaphoreType.DMA((out_weight.shape[0] // DEEP,)),
        ],
        pl.CostEstimate(flops=2 * 10**9, bytes_accessed=8 * 10**6, transcendentals=0),
        28,
    )(core, attention, in_hbm(out_weight))
    got = lax.ppermute(other, "tp", [(i, i ^ 1) for i in range(8)])
    block = half // 4
    own, *parts = call(
        pair_kernel, [((block, columns), F32)] + [((block, columns), BF16)] * 3, [SMEM, VMEM, VMEM]
    )(y, mine, got)
    arrived = [
        lax.ppermute(part, "tp", [(i, (i + 2 * k) % 8) for i in range(8)])
        for k, part in ((2, parts[1]), (1, parts[0]), (3, parts[2]))
    ]
    return call(sum_kernel, [((block, columns), BF16)], [VMEM] * 4)(own, *arrived)


def solution(mesh):
    placed = (
        P("pfx", "tp"),
        P("pfx"),
        P(),
        P("pfx"),
        P("pfx", "tp"),
        P("pfx", "tp"),
        P("pfx", None, "tp"),
        P("pfx", None, "tp"),
        P("tp", "pfx"),
    )
    return jax.shard_map(
        on_device, mesh=mesh, in_specs=placed, out_specs=P("tp", "pfx"), check_vma=False
    )
```

```python
import functools

import jax
import jax.numpy as jnp
from jax import lax
from jax.experimental import pallas as pl
from jax.experimental.pallas import tpu as pltpu
from jax.sharding import PartitionSpec as P

HDIM = 128
SLOTS = 8
EXTRA = 128
CAP = 6
LOG2E = 1.4426950408889634
LN2 = 0.6931471805599453
F32 = jnp.float32
BF16 = jnp.bfloat16
VMEM = pl.BlockSpec(memory_space=pltpu.VMEM)
SMEM = pl.BlockSpec(memory_space=pltpu.SMEM)
HBM = pl.BlockSpec(memory_space=pltpu.HBM)
NT = (((1,), (1,)), ((), ()))


def iota(shape, dim):
    return lax.broadcasted_iota(jnp.int32, shape, dim)


def one_hot(condition):
    return jnp.where(condition, 1.0, 0.0).astype(BF16)


def dest_rows(route_ref, place_ref, count_ref, add):
    for owner in range(place_ref.shape[0]):
        count_ref[owner] = 0
    for r in range(route_ref.shape[0]):
        owner = place_ref[route_ref[r]]
        rank = count_ref[owner]
        count_ref[owner] = rank + 1
        add(r, owner * SLOTS + rank)


def pack_kernel(route_in, place_in, q_in, out_ref, route_ref, place_ref, q_ref, count_ref, sems):
    rows = q_ref.shape[0]
    pairs = [(route_in, route_ref), (place_in, place_ref), (q_in, q_ref)]
    loads = [pltpu.make_async_copy(a, b, sems.at[i]) for i, (a, b) in enumerate(pairs)]
    for load in loads:
        load.start()
    for load in loads[:2]:
        load.wait()
    lane = iota((SLOTS, 128), 1)
    dest = [jnp.full((SLOTS, 128), -1, jnp.int32)]

    def add(r, row):
        dest[0] = jnp.where(lane == r, row, dest[0])

    dest_rows(route_ref, place_ref, count_ref, add)
    buffer_rows, wide = out_ref.shape[0], SLOTS * rows
    place = jnp.concatenate([dest[0][:1, :rows]] * SLOTS, axis=1)
    row, lane = iota((buffer_rows, wide), 0), iota((buffer_rows, wide), 1)
    owner = row // SLOTS * SLOTS
    fits = row % SLOTS == lane // rows
    count = jnp.dot(
        one_hot(dest[0][:1, :rows] // SLOTS * SLOTS == owner[:, :rows]),
        jnp.ones((rows, EXTRA), BF16),
        preferred_element_type=F32,
    )
    out_ref[:, CAP * 2 * HDIM :] = count.astype(BF16)
    loads[2].wait()
    stacked = by_half(q_ref)
    picks = [one_hot(fits & (place == owner + k)) for k in range(CAP)]
    out = jnp.dot(jnp.concatenate(picks, axis=0), stacked, preferred_element_type=F32)
    for k in range(CAP):
        out_ref[:, k * 2 * HDIM : (k + 1) * 2 * HDIM] = out[
            k * buffer_rows : (k + 1) * buffer_rows
        ].astype(BF16)


def by_half(ref):
    parts = []
    for sub in range(SLOTS):
        low, high = sub * HDIM, (SLOTS + sub) * HDIM
        parts.append(
            jnp.concatenate([ref[:, low : low + HDIM], ref[:, high : high + HDIM]], axis=1)
        )
    return jnp.concatenate(parts, axis=0)


def by_slot(ref):
    return jnp.concatenate(
        [ref[:, k * 2 * HDIM : (k + 1) * 2 * HDIM] for k in range(CAP)], axis=0
    )


def suffix_kernel(
    route_ref,
    place_ref,
    len_ref,
    q_ref,
    k_in,
    v_in,
    out_ref,
    lse_ref,
    dest_ref,
    k_ref,
    v_ref,
    count_ref,
    sems,
):
    requests, cache, depth = k_ref.shape
    heads = q_ref.shape[1] // depth
    batch = 16
    loads = []
    for b in range(requests // batch):
        sl = pl.ds(b * batch, batch)
        loads.append(pltpu.make_async_copy(k_in.at[sl], k_ref.at[sl], sems.at[0, b]))
        loads.append(pltpu.make_async_copy(v_in.at[sl], v_ref.at[sl], sems.at[1, b]))
    for load in loads:
        load.start()
    dest = [jnp.zeros((requests, 128), jnp.int32)]
    row = iota((requests, 128), 0)

    def add(r, place):
        dest[0] = jnp.where(row == r, place, dest[0])

    dest_rows(route_ref, place_ref, count_ref, add)
    dest_ref[...] = dest[0]
    for b in range(requests // batch):
        first = b * batch
        sl = slice(first, first + batch)
        q = jnp.concatenate([q_ref[sl, h * depth : (h + 1) * depth] for h in range(heads)], axis=0)
        own = iota((batch, 128), 0)
        live = jnp.zeros((batch, 128), jnp.int32)
        for r in range(batch):
            live = jnp.where(own == r, len_ref[first + r], live)
        loads[2 * b].wait()
        loads[2 * b + 1].wait()
        keys = k_ref[sl].reshape(batch * cache, depth)
        values = v_ref[sl].reshape(batch * cache, depth)
        scores = lax.dot_general(q, keys, NT, preferred_element_type=F32)
        column = iota((batch, batch * cache), 1)
        start = iota((batch, batch * cache), 0) * cache
        inside = (column >= start) & (column < start + live[:, :1])
        bias = jnp.where(inside, 0.0, -jnp.inf)
        scores = scores * (depth**-0.5 * LOG2E) + jnp.concatenate([bias] * heads, axis=0)
        top = jnp.max(scores, axis=1, keepdims=True)
        weights = jnp.exp2(scores - top).astype(BF16)
        both = jnp.dot(
            weights,
            jnp.concatenate([values, jnp.ones_like(values)], axis=1),
            preferred_element_type=F32,
        )
        total = both[:, depth:]
        out = both[:, :depth] / total
        lse = top * LN2 + jnp.log(total)
        for h in range(heads):
            part = slice(h * batch, (h + 1) * batch)
            out_ref[sl, h * depth : (h + 1) * depth] = out[part]
            lse_ref[sl, h * depth : (h + 1) * depth] = lse[part]


CHUNKS = (1024, 3072, 4096)
GROUP = 32


def prefix_kernel(recv_ref, k_in, v_in, out_ref, k_ref, v_ref, q_ref, acc_ref, top_ref, sems):
    depth = k_ref.shape[1]
    buffer_rows = recv_ref.shape[0]
    width = CAP * 2 * depth
    heads = 2 * SLOTS
    cols = heads * GROUP
    items = buffer_rows // SLOTS * CAP
    blocks = items // GROUP
    steps = len(CHUNKS)
    spans = [slice(sum(CHUNKS[:i]), sum(CHUNKS[: i + 1])) for i in range(steps)]
    loads = [
        [
            pltpu.make_async_copy(k_in.at[sl, :], k_ref.at[sl, :], sems.at[0, i]),
            pltpu.make_async_copy(v_in.at[sl, :], v_ref.at[sl, :], sems.at[1, i]),
        ]
        for i, sl in enumerate(spans)
    ]
    for load in loads[0]:
        load.start()

    square = (buffer_rows, buffer_rows)
    row, other = iota(square, 0), iota(square, 1)
    number = recv_ref[:, width:]
    first = (other % SLOTS == 0) & (other // SLOTS < row // SLOTS)
    first_turned = (row % SLOTS == 0) & (row // SLOTS < other // SLOTS)
    turn = (((0,), (0,)), ((), ()))
    base_down = jnp.dot(one_hot(first), number, preferred_element_type=F32)
    base_across = lax.dot_general(number, one_hot(first_turned), turn, preferred_element_type=F32)
    number_across = lax.dot_general(number, one_hot(row == other), turn, preferred_element_type=F32)
    number_down = number.astype(F32)
    used = jnp.max(base_down + number_down).astype(jnp.int32)
    active = jnp.minimum((used + GROUP - 1) // GROUP, blocks)
    place_down = [
        jnp.where(number_down > k, base_down + k, -1.0).astype(jnp.int32) for k in range(CAP)
    ]
    place_across = jnp.concatenate(
        [
            jnp.where(number_across[:1] > k, base_across[:1] + k, -1.0).astype(jnp.int32)
            for k in range(CAP)
        ],
        axis=1,
    )

    scale = depth**-0.5 * LOG2E
    received = by_slot(recv_ref)
    shape = (items, CAP * buffer_rows)
    found = place_across == iota(shape, 0)
    picks = [one_hot(found & (iota(shape, 1) % SLOTS == sub)) for sub in range(SLOTS)]
    q = jnp.dot(jnp.concatenate(picks, axis=0), received, preferred_element_type=F32).astype(BF16)
    for sub in range(SLOTS):
        for b in range(blocks):
            of = slice(sub * items + b * GROUP, sub * items + (b + 1) * GROUP)
            for half in range(2):
                start = b * cols + (half * SLOTS + sub) * GROUP
                q_ref[start : start + GROUP, :] = q[of, half * depth : (half + 1) * depth]

    def scores_of(span, c):
        q = q_ref[c * cols : (c + 1) * cols, :]
        return lax.dot_general(k_ref[span, :], q, NT, preferred_element_type=F32) * scale

    def value_rows(span):
        values = v_ref[span, :]
        return jnp.concatenate([values.T, jnp.ones((16, values.shape[0]), BF16)], axis=0)

    for c in range(blocks):
        start = jnp.where(c < active, 0.0, 1.0)
        acc_ref[:, c * cols : (c + 1) * cols] = jnp.full((acc_ref.shape[0], cols), start, F32)

    def attend(block):
        for i, span in enumerate(spans):
            for load in loads[i]:
                load.wait()
            if i + 1 < steps:
                for load in loads[i + 1]:
                    load.start()
            turned = value_rows(span)
            for c in range(blocks):

                def body(c=c, span=span, turned=turned):
                    weights = jnp.exp2(scores_of(span, c)).astype(BF16)
                    acc_ref[:, c * cols : (c + 1) * cols] += jnp.dot(
                        turned, weights, preferred_element_type=F32
                    )

                block(c, body)

    @pl.when(active == blocks)
    def _():
        attend(lambda c, body: body())

    @pl.when(active < blocks)
    def _():
        attend(lambda c, body: pl.when(c < active)(body))

    top_ref[...] = jnp.zeros_like(top_ref)
    total = acc_ref[depth : depth + 1, :]
    fine = (total > 2.0**-64) & (total < 2.0**100)

    @pl.when(jnp.min(jnp.where(fine, 1.0, 0.0)) < 0.5)
    def _():
        for c in range(blocks):
            sl = slice(c * cols, (c + 1) * cols)

            def find(i, top):
                span = pl.ds(pl.multiple_of(i * CHUNKS[0], CHUNKS[0]), CHUNKS[0])
                return jnp.maximum(top, jnp.max(scores_of(span, c), axis=0, keepdims=True))

            again_steps = k_ref.shape[0] // CHUNKS[0]
            top = lax.fori_loop(0, again_steps, find, jnp.full((1, cols), -jnp.inf, F32))
            top_ref[:, sl] = jnp.broadcast_to(top, (8, cols))
            acc_ref[:, sl] = jnp.zeros((acc_ref.shape[0], cols), F32)

            def again(i, carry):
                span = pl.ds(pl.multiple_of(i * CHUNKS[0], CHUNKS[0]), CHUNKS[0])
                weights = jnp.exp2(scores_of(span, c) - top).astype(BF16)
                acc_ref[:, sl] += jnp.dot(value_rows(span), weights, preferred_element_type=F32)
                return carry

            lax.fori_loop(0, again_steps, again, 0)

    total = acc_ref[depth : depth + 1, :]
    inverse = 1.0 / total
    lse = top_ref[:1, :] * LN2 + jnp.log(total)
    high = lse.astype(BF16).astype(F32)
    middle = (lse - high).astype(BF16).astype(F32)
    low = lse - high - middle
    wide = iota((8, blocks * cols), 0)
    pieces = jnp.where(
        wide == 0, high, jnp.where(wide == 1, middle, jnp.where(wide == 2, low, 0.0))
    ).astype(BF16)
    four = depth // GROUP
    outs = []
    for h0 in range(0, heads, four):
        turned = []
        for b in range(blocks):
            sl = slice(b * cols + h0 * GROUP, b * cols + (h0 + four) * GROUP)
            turned.append((acc_ref[:depth, sl] * inverse[:, sl]).astype(BF16).T)
        for h in range(four):
            outs.append(
                jnp.concatenate([x[h * GROUP : (h + 1) * GROUP] for x in turned], axis=0)
            )
    results = jnp.concatenate(
        [
            jnp.concatenate([outs[sub], outs[SLOTS + sub]], axis=1)
            for sub in range(SLOTS)
        ],
        axis=0,
    )
    shape = (buffer_rows, SLOTS * items)
    same = iota(shape, 0) % SLOTS == iota(shape, 1) // items
    item = iota(shape, 1) % items
    picks = [
        one_hot(same & (jnp.concatenate([place] * (shape[1] // EXTRA), axis=1) == item))
        for place in place_down
    ]
    out = jnp.dot(jnp.concatenate(picks, axis=0), results, preferred_element_type=F32)
    for k in range(CAP):
        out_ref[:, k * 2 * depth : (k + 1) * 2 * depth] = out[
            k * buffer_rows : (k + 1) * buffer_rows
        ].astype(BF16)
    spread = (EXTRA, cols)
    same_head = iota(spread, 0) // 8 == iota(spread, 1) // GROUP
    to_item = one_hot(iota((GROUP, cols), 1) % GROUP == iota((GROUP, cols), 0))
    listed = []
    for b in range(blocks):
        part = pieces[:, b * cols : (b + 1) * cols]
        by_head = jnp.where(same_head, jnp.concatenate([part] * heads, axis=0), 0.0).astype(BF16)
        listed.append(lax.dot_general(to_item, by_head, NT, preferred_element_type=F32))
    listed = jnp.concatenate(listed, axis=0).astype(BF16)
    own = row % SLOTS == other // 8 % SLOTS
    to_row = [one_hot(place[:, :items] == iota((buffer_rows, items), 1)) for place in place_down]
    rows_of = jnp.dot(jnp.concatenate(to_row, axis=0), listed, preferred_element_type=F32)
    ones, lanes = [], []
    for k in range(CAP):
        one = rows_of[k * buffer_rows : (k + 1) * buffer_rows]
        ones.append(jnp.where(own, one, 0.0).astype(BF16))
        to_lane = (other // 16 == k) & (other // 8 % 2 == row // 64) & (other % 8 == row % 8)
        lanes.append(one_hot(to_lane))
    tail = jnp.dot(
        jnp.concatenate(ones, axis=1), jnp.concatenate(lanes, axis=0), preferred_element_type=F32
    )
    out_ref[:, width:] = tail.astype(BF16)


def merge_kernel(back_ref, dest_ref, suffix_ref, lse_ref, out_ref, merged_ref, sems):
    copies, requests, _ = out_ref.shape
    buffer_rows = back_ref.shape[0]
    dest = dest_ref[:, :1]
    returned = by_slot(back_ref)
    shape = (requests, CAP * buffer_rows)
    lane = iota(shape, 1)
    mine = lane % buffer_rows // SLOTS * SLOTS + lane // buffer_rows == dest
    short = (requests, buffer_rows)
    group = iota(short, 1) // SLOTS == dest // SLOTS
    slot = iota(short, 1) // 16 == dest % SLOTS
    wide = (EXTRA, 2 * HDIM)
    to_half = one_hot((iota(wide, 0) // 8 % 2 == iota(wide, 1) // HDIM) & (iota(wide, 0) % 8 < 3))
    picks = [one_hot(mine & (lane % SLOTS == sub)) for sub in range(SLOTS)]
    prefixes = jnp.dot(jnp.concatenate(picks, axis=0), returned, preferred_element_type=F32)
    picks = [one_hot(group & (iota(short, 1) % SLOTS == sub)) for sub in range(SLOTS)]
    pieces = jnp.dot(
        jnp.concatenate(picks, axis=0), back_ref[:, CAP * 2 * HDIM :], preferred_element_type=F32
    )
    pieces = jnp.where(jnp.concatenate([slot] * SLOTS, axis=0), pieces, 0.0).astype(BF16)
    lses = jnp.dot(pieces, to_half, preferred_element_type=F32)
    sends = []
    for half in range(2):
        part = slice(half * HDIM, (half + 1) * HDIM)
        for sub in range(SLOTS):
            rows = slice(sub * requests, (sub + 1) * requests)
            start = (half * SLOTS + sub) * HDIM
            sl = slice(start, start + HDIM)
            prefix_lse = lses[rows, part]
            suffix_lse = lse_ref[:, sl]
            top = jnp.maximum(prefix_lse, suffix_lse)
            prefix_part = jnp.exp(prefix_lse - top)
            suffix_part = jnp.exp(suffix_lse - top)
            merged = (prefix_part * prefixes[rows, part] + suffix_part * suffix_ref[:, sl]) / (
                prefix_part + suffix_part
            )
            merged_ref[:, sl] = merged.astype(BF16)
        columns = pl.ds(half * SLOTS * HDIM, SLOTS * HDIM)
        for copy in range(copies):
            send = pltpu.make_async_copy(
                merged_ref.at[:, columns], out_ref.at[copy, :, columns], sems.at[half, copy]
            )
            send.start()
            sends.append(send)
    for send in sends:
        send.wait()


DEEP = 512
TILE = 256


def project_kernel(core_ref, a_ref, w_in, mine_ref, other_ref, w_ref, acc_ref, sems):
    steps = w_ref.shape[0] // DEEP
    loads = []
    for n in range(steps):
        sl = pl.ds(n * DEEP, DEEP)
        loads.append(pltpu.make_async_copy(w_in.at[sl, :], w_ref.at[sl, :], sems.at[n]))
        loads[n].start()
    core = core_ref[0]
    block = a_ref.shape[0] // 8
    half = 4 * block
    order = [(y, core) for y in range(4)] + [(y, 1 - core) for y in range(4)]
    a = jnp.concatenate(
        [a_ref[pl.ds(pl.multiple_of((2 * y + c) * block, block), block), :] for y, c in order],
        axis=0,
    )
    for n in range(steps):
        loads[n].wait()
        deep = slice(n * DEEP, (n + 1) * DEEP)
        for t in range(w_ref.shape[1] // TILE):
            sl = slice(t * TILE, (t + 1) * TILE)
            out = jnp.dot(a[:, deep], w_ref[deep, sl], preferred_element_type=F32)
            if n > 0:
                out += acc_ref[:, sl]
            if n + 1 < steps:
                acc_ref[:, sl] = out
            else:
                mine_ref[:, sl] = out[:half]
                other_ref[:, sl] = out[half:].astype(BF16)


def pair_kernel(y_ref, mine_ref, got_ref, own_ref, one_ref, two_ref, three_ref):
    y = y_ref[0]
    block = own_ref.shape[0]

    def part(k):
        start = pl.multiple_of(lax.rem(y + k, 4) * block, block)
        return mine_ref[pl.ds(start, block), :] + got_ref[pl.ds(start, block), :].astype(F32)

    one_ref[...] = part(1).astype(BF16)
    two_ref[...] = part(2).astype(BF16)
    three_ref[...] = part(3).astype(BF16)
    own_ref[...] = part(0)


def sum_kernel(own_ref, one_ref, two_ref, three_ref, out_ref):
    out_ref[...] = (
        own_ref[...]
        + one_ref[...].astype(F32)
        + two_ref[...].astype(F32)
        + three_ref[...].astype(F32)
    ).astype(BF16)


def in_hbm(array):
    return pltpu.with_memory_space_constraint(array, pltpu.HBM)


def call(kernel, outs, specs, scratch=(), cost=None, mib=16):
    shapes = [jax.ShapeDtypeStruct(shape, dtype) for shape, dtype in outs]
    many = len(shapes) > 1
    return pl.pallas_call(
        kernel,
        out_shape=shapes if many else shapes[0],
        in_specs=specs,
        out_specs=[VMEM] * len(shapes) if many else VMEM,
        scratch_shapes=list(scratch),
        compiler_params=pltpu.CompilerParams(vmem_limit_bytes=mib * 2**20),
        cost_estimate=cost,
    )


def on_device(
    queries, route, place, suffix_len, prefix_keys, prefix_values, suffix_keys, suffix_values, out_weight
):
    requests, width = queries.shape
    owners = lax.axis_size("pfx")
    heads = width // HDIM
    buffer_rows = owners * SLOTS
    rows = owners * CAP * heads
    count = pltpu.SMEM((owners,), jnp.int32)
    tp = lax.axis_index("tp")
    core, y = (tp % 2).reshape(1), (tp // 2).reshape(1)

    def exchange(x):
        shape = x.shape
        x = x.reshape(owners, -1, shape[1])
        x = lax.all_to_all(x, "pfx", split_axis=0, concat_axis=0, tiled=True)
        return x.reshape(shape)

    packed = call(
        pack_kernel,
        [((buffer_rows, CAP * 2 * HDIM + EXTRA), BF16)],
        [HBM, HBM, HBM],
        [
            pltpu.SMEM(route.shape, jnp.int32),
            pltpu.SMEM(place.shape, jnp.int32),
            pltpu.VMEM(queries.shape, BF16),
            count,
            pltpu.SemaphoreType.DMA((3,)),
        ],
        None,
        62,
    )(in_hbm(route), in_hbm(place), in_hbm(queries))
    received = exchange(packed)
    suffix_out, suffix_lse, dest = call(
        suffix_kernel,
        [((requests, width), F32), ((requests, width), F32), ((requests, 128), jnp.int32)],
        [SMEM, SMEM, SMEM, VMEM, HBM, HBM],
        [
            pltpu.VMEM(suffix_keys.shape, BF16),
            pltpu.VMEM(suffix_values.shape, BF16),
            count,
            pltpu.SemaphoreType.DMA((2, 2)),
        ],
        pl.CostEstimate(flops=2 * 10**9, bytes_accessed=5 * 10**6, transcendentals=2 * 10**6),
        32,
    )(route, place, suffix_len, queries, in_hbm(suffix_keys), in_hbm(suffix_values))
    prefix = call(
        prefix_kernel,
        [((buffer_rows, CAP * 2 * HDIM + EXTRA), BF16)],
        [VMEM, HBM, HBM],
        [
            pltpu.VMEM(prefix_keys.shape, BF16),
            pltpu.VMEM(prefix_values.shape, BF16),
            pltpu.VMEM((rows, HDIM), BF16),
            pltpu.VMEM((HDIM + 16, rows), F32),
            pltpu.VMEM((8, rows), F32),
            pltpu.SemaphoreType.DMA((2, len(CHUNKS))),
        ],
        pl.CostEstimate(flops=10**10, bytes_accessed=5 * 10**6, transcendentals=12 * 10**6),
        44,
    )(received, in_hbm(prefix_keys), in_hbm(prefix_values))
    back = exchange(prefix)
    copies = pl.pallas_call(
        merge_kernel,
        out_shape=pltpu.HBM((owners, requests, width), BF16),
        in_specs=[VMEM] * 4,
        out_specs=HBM,
        scratch_shapes=[
            pltpu.VMEM((requests, width), BF16),
            pltpu.SemaphoreType.DMA((2, owners)),
        ],
        compiler_params=pltpu.CompilerParams(vmem_limit_bytes=16 * 2**20),
    )(back, dest, suffix_out, suffix_lse)
    attention = exchange(copies.reshape(owners * requests, width))
    columns = out_weight.shape[1]
    half = owners * requests // 2
    mine, other = call(
        project_kernel,
        [((half, columns), F32), ((half, columns), BF16)],
        [SMEM, VMEM, HBM],
        [
            pltpu.VMEM(out_weight.shape, BF16),
            pltpu.VMEM((2 * half, columns), F32),
            pltpu.SemaphoreType.DMA((out_weight.shape[0] // DEEP,)),
        ],
        pl.CostEstimate(flops=2 * 10**9, bytes_accessed=8 * 10**6, transcendentals=0),
        28,
    )(core, attention, in_hbm(out_weight))
    got = lax.ppermute(other, "tp", [(i, i ^ 1) for i in range(8)])
    block = half // 4
    own, *parts = call(
        pair_kernel, [((block, columns), F32)] + [((block, columns), BF16)] * 3, [SMEM, VMEM, VMEM]
    )(y, mine, got)
    arrived = [
        lax.ppermute(part, "tp", [(i, (i + 2 * k) % 8) for i in range(8)])
        for k, part in ((2, parts[1]), (1, parts[0]), (3, parts[2]))
    ]
    return call(sum_kernel, [((block, columns), BF16)], [VMEM] * 4)(own, *arrived)


def solution(mesh):
    placed = (
        P("pfx", "tp"),
        P("pfx"),
        P(),
        P("pfx"),
        P("pfx", "tp"),
        P("pfx", "tp"),
        P("pfx", None, "tp"),
        P("pfx", None, "tp"),
        P("tp", "pfx"),
    )
    return jax.shard_map(
        on_device, mesh=mesh, in_specs=placed, out_specs=P("tp", "pfx"), check_vma=False
    )
```
